512 devices in a mesh: ctx: 32 (over y, x, core), head: 16 (over z).
Axes of the slice: x: 4, y: 4, z: 16, core: 2. Of those that a mesh axis runs over, the one named last changes fastest.
Arguments:
- query: bfloat16 [4096, 12288], P('ctx', 'head'), may hold values from -128 to 128
- kv_row: bfloat16 [4096, 576], P('ctx'), may hold values from -64 to 64
- w_uk: bfloat16 [512, 8192], P(None, 'head'), may hold values from -0.25 to 0.25
- w_uv: bfloat16 [512, 8192], P(None, 'head'), may hold values from -0.25 to 0.25
- grad_out: bfloat16 [4096, 8192], P('ctx', 'head'), may hold values from -6 to 6
- block_start: int32 [64], replicated, may hold values from 0 to 4032, as said below
Outputs:
- grad_query: bfloat16 [4096, 12288], P('ctx', 'head')
- grad_kv_row: float32 [4096, 576], P('ctx')
- grad_w_uk: float32 [512, 8192], P('ctx', 'head')
- grad_w_uv: float32 [512, 8192], P('ctx', 'head')
The draws below stay inside these ranges and needn't reach their ends.
Inputs may be any that keep to these rules, and one draw needn't show every extreme that they name: block_start is a permutation of the multiples of 64 below 4096, so every position occurs once.
All inputs are finite; a program needn't handle non-finite values.
Results may differ from the reference program's by a relative error of at most 0.02.
Values may be sent and summed in bfloat16 or wider, within the bound.
No kernel may reach another device: no remote copies, remote signals or barrier semaphores. Data moves between devices by JAX's collectives and lax.ppermute only.
A program may use at most 128 MiB of HBM per device.

```python
import math
import jax
import jax.numpy as jnp
from jax import lax

LATENT = 512
ROPE = 64
NOPE = 128
VDIM = 128
HEADS = 64
TOK_DEV = 128
HALF = 64
TOKENS = 4096
N_CTX = 32


def rope_parts(key):
    base_key = jax.random.fold_in(key, 7)
    base = jax.random.truncated_normal(base_key, -6.0, 6.0, (TOKENS, ROPE), jnp.float32)
    return base


def draw_kv_row(key, part):
    base = rope_parts(key)
    key = jax.random.fold_in(key, 2)
    first_key, second_key = jax.random.split(key)
    latent = jax.random.truncated_normal(first_key, -6.0, 6.0, (TOKENS, LATENT), jnp.float32)
    scales = jnp.exp(jax.random.uniform(second_key, (TOKENS, 1), jnp.float32, 0.0, math.log(10.0)))
    rope = base
    return jnp.concatenate([latent * scales, rope], axis=1).astype(jnp.bfloat16)


def draw_query(key, part):
    key = jax.random.fold_in(key, 3)
    width = NOPE + ROPE
    values = jax.random.truncated_normal(key, -6.0, 6.0, (TOKENS, HEADS, width), jnp.float32)
    return values.reshape(TOKENS, HEADS * width).astype(jnp.bfloat16)


def draw_block_start(key, part):
    key = jax.random.fold_in(key, 5)
    number = TOKENS // HALF
    return (jax.random.permutation(key, number) * HALF).astype(jnp.int32)


def block_scale(own_key, dims, cuts, least, high):
    loudness, own = 1.0, jax.random.fold_in(own_key, 6)
    for position, blocks in cuts:
        heights = jnp.exp(jax.random.uniform(jax.random.fold_in(own, position), (blocks,), jnp.float32, least / len(cuts), high / len(cuts)))
        loudness = loudness * jnp.repeat(heights, dims[position] // blocks).reshape([-1 if axis == position else 1 for axis in range(len(dims))])
    return loudness


def gaussian(key, extent, scale, reach, cuts=(), kind=jnp.bfloat16):
    loudness = block_scale(key, extent, cuts, -0.22, 0.18) if cuts else 1.0
    array = jax.random.normal(key, extent, jnp.float32) * scale * loudness
    return jnp.minimum(jnp.maximum(array, -reach), reach).astype(kind)


def setup_inputs(seed: int = 0) -> dict:
    key_of = jax.random.split(jax.random.key(seed), 7)
    return {
        "query": draw_query(jax.random.fold_in(key_of[6], 71), 0),
        "kv_row": draw_kv_row(jax.random.fold_in(key_of[6], 71), 0),
        "w_uk": gaussian(key_of[2], (LATENT, HEADS * NOPE), LATENT ** -0.5, 0.25, ((1, 16),)),
        "w_uv": gaussian(key_of[3], (LATENT, HEADS * VDIM), LATENT ** -0.5, 0.25, ((1, 16),)),
        "grad_out": gaussian(key_of[4], (TOKENS, HEADS * VDIM), 1.0, 6.0, ((0, 32), (1, 16))),
        "block_start": draw_block_start(jax.random.fold_in(key_of[6], 71), 0),
    }


eps = 1e-06

def rms_rows(latent):
    values = latent.astype(jnp.float32)
    inverse = lax.rsqrt(lax.optimization_barrier(jnp.mean(values * values, axis=-1, keepdims=True)) + eps)
    return (values * inverse, inverse)

def shard_terms(left, right):
    left_parts = left.reshape(N_CTX, TOK_DEV, left.shape[1])
    right_parts = right.reshape(N_CTX, TOK_DEV, right.shape[1])

    def one_shard(pair):
        return jnp.dot(pair[0].T, pair[1], preferred_element_type=jnp.float32).astype(jnp.bfloat16)
    stacked = lax.map(one_shard, (left_parts, right_parts))
    stacked = lax.optimization_barrier(stacked)
    return lax.optimization_barrier(jnp.sum(stacked.astype(jnp.float32), axis=0))

def reference(query, kv_row, w_uk, w_uv, grad_out, block_start):
    width_q = NOPE + ROPE
    scale = 1.0 / math.sqrt(width_q)
    block = min(512, TOKENS)
    offsets = jnp.arange(HALF, dtype=jnp.int32)
    positions = (block_start[:, None] + offsets[None, :]).reshape(-1).astype(jnp.int32)
    order = jnp.argsort(positions).astype(jnp.int32)
    q_sorted = jnp.take(query, order, axis=0).reshape(TOKENS, HEADS, width_q)
    go_sorted = jnp.take(grad_out, order, axis=0).reshape(TOKENS, HEADS, VDIM)
    rows = jnp.take(kv_row, order, axis=0)
    x_hat, inverse = rms_rows(rows[:, :LATENT])
    normed = x_hat.astype(jnp.bfloat16)
    keys_nope = jnp.dot(normed, w_uk, preferred_element_type=jnp.float32).astype(jnp.bfloat16).reshape(TOKENS, HEADS, NOPE)
    values = jnp.dot(normed, w_uv, preferred_element_type=jnp.float32).astype(jnp.bfloat16).reshape(TOKENS, HEADS, VDIM)
    k_rope = rows[:, LATENT:]

    def one_head(items):
        q_head, go_head, kn_head, v_head = items
        pieces = []
        key_grad = jnp.zeros((TOKENS, NOPE), jnp.float32)
        rope_grad = jnp.zeros((TOKENS, ROPE), jnp.float32)
        value_grad = jnp.zeros((TOKENS, VDIM), jnp.float32)
        for index in range(TOKENS // block):
            low = index * block
            high = low + block
            q_nope = q_head[low:high, :NOPE]
            q_rope = q_head[low:high, NOPE:]
            go_block = go_head[low:high]
            k_nope = kn_head[:high]
            k_part = k_rope[:high]
            v_part = v_head[:high]
            scores = (jnp.dot(q_nope, k_nope.T, preferred_element_type=jnp.float32) + jnp.dot(q_rope, k_part.T, preferred_element_type=jnp.float32)) * scale
            visible = jnp.arange(high)[None, :] <= (low + jnp.arange(block))[:, None]
            top = lax.optimization_barrier(jnp.max(jnp.where(visible, scores, -jnp.inf), axis=-1, keepdims=True))
            log_total = top + jnp.log(lax.optimization_barrier(jnp.sum(jnp.where(visible, jnp.exp(scores - top), 0.0), axis=-1, keepdims=True)))
            slopes = jnp.dot(go_block, v_part.T, preferred_element_type=jnp.float32)
            probs = jnp.where(visible, jnp.exp(scores - log_total), 0.0)
            average = lax.optimization_barrier(jnp.sum(probs * slopes, axis=-1, keepdims=True))
            score_grad = (probs * (slopes - average) * scale).astype(jnp.bfloat16)
            pieces.append(jnp.concatenate([jnp.dot(score_grad, k_nope, preferred_element_type=jnp.float32), jnp.dot(score_grad, k_part, preferred_element_type=jnp.float32)], axis=1).astype(jnp.bfloat16))
            key_grad = key_grad.at[:high].add(jnp.dot(score_grad.T, q_nope, preferred_element_type=jnp.float32))
            rope_grad = rope_grad.at[:high].add(jnp.dot(score_grad.T, q_rope, preferred_element_type=jnp.float32))
            value_grad = value_grad.at[:high].add(jnp.dot(probs.astype(jnp.bfloat16).T, go_block, preferred_element_type=jnp.float32))
        return (jnp.concatenate(pieces, axis=0), key_grad, rope_grad, value_grad)
    grad_q, key_grad, rope_grad, value_grad = lax.map(one_head, (jnp.moveaxis(q_sorted, 1, 0), jnp.moveaxis(go_sorted, 1, 0), jnp.moveaxis(keys_nope, 1, 0), jnp.moveaxis(values, 1, 0)))
    grad_q_sorted = jnp.moveaxis(grad_q, 0, 1).reshape(TOKENS, HEADS * width_q)
    key_flat = jnp.moveaxis(key_grad, 0, 1).reshape(TOKENS, HEADS * NOPE).astype(jnp.bfloat16)
    value_flat = jnp.moveaxis(value_grad, 0, 1).reshape(TOKENS, HEADS * VDIM).astype(jnp.bfloat16)
    rope_total = lax.optimization_barrier(jnp.sum(rope_grad, axis=0))
    latent_grad = jnp.dot(key_flat, w_uk.T, preferred_element_type=jnp.float32) + jnp.dot(value_flat, w_uv.T, preferred_element_type=jnp.float32)
    grad_latent = inverse * (latent_grad - x_hat * lax.optimization_barrier(jnp.mean(latent_grad * x_hat, axis=-1, keepdims=True)))
    rows_sorted = jnp.concatenate([grad_latent, rope_total], axis=1)
    grad_query = jnp.zeros_like(grad_q_sorted).at[order].set(grad_q_sorted)
    grad_kv_row = jnp.zeros_like(rows_sorted).at[order].set(rows_sorted)
    key_orig = jnp.zeros_like(key_flat).at[order].set(key_flat)
    value_orig = jnp.zeros_like(value_flat).at[order].set(value_flat)
    normed_orig = rms_rows(kv_row[:, :LATENT])[0].astype(jnp.bfloat16)
    grad_w_uk = shard_terms(normed_orig, key_orig)
    grad_w_uv = shard_terms(normed_orig, value_orig)
    return (grad_query, grad_kv_row, grad_w_uk, grad_w_uv)
```

```python
import functools
import math

import jax
import jax.numpy as jnp
from jax import lax
from jax.experimental import pallas as pl
from jax.experimental.pallas import tpu as pltpu
from jax.sharding import PartitionSpec as P

LATENT = 512
ROPE = 64
NOPE = 128
VDIM = 128
WIDTH_Q = NOPE + ROPE
HALF = 64
HEADS = 4
CHIPS = 16
SIDE = 4
PIECE = HALF // SIDE
ROWS = 2 * HALF
KEYS = 4096
QUERIES = 2 * CHIPS * PIECE
KEY_ROWS = 2 * ROWS + HALF
IN_ROWS = KEY_ROWS + 5 * PIECE
OUT_ROWS = KEY_ROWS + 3 * PIECE
CHUNK = 512
GROUP = 256
N_CHUNKS = KEYS // CHUNK
N_GROUPS = QUERIES // GROUP
Z_WIDTH = 640
LOG2E = 1.4426950408889634
SCALE = 1.0 / math.sqrt(WIDTH_Q)

eps = 1e-06
masked_low = -1e30
bf16 = jnp.bfloat16
f32 = jnp.float32
VMEM = pl.BlockSpec(memory_space=pltpu.VMEM)
SMEM = pl.BlockSpec(memory_space=pltpu.SMEM)


def dot(left, right, left_dim=1, right_dim=0):
    return lax.dot_general(
        left, right, (((left_dim,), (right_dim,)), ((), ())), preferred_element_type=f32
    )


def rms_rows(latent):
    values = latent.astype(f32)
    inverse = lax.rsqrt(jnp.mean(values * values, axis=-1, keepdims=True) + eps)
    return (values * inverse, inverse)


def expand_kernel(kv_ref, wk_ref, wv_ref, q_ref, g_ref, out_ref):
    normed = rms_rows(kv_ref[:, :LATENT])[0].astype(bf16)
    keys = dot(normed, wk_ref[...]).astype(bf16)
    values = dot(normed, wv_ref[...]).astype(bf16)
    rope = kv_ref[:, LATENT:]
    rope = jnp.concatenate([rope[:HALF], rope[HALF:]], axis=1)
    for x in range(HEADS):
        key = keys[:, x * NOPE : (x + 1) * NOPE]
        value = values[:, x * VDIM : (x + 1) * VDIM]
        q_nope = q_ref[:, x * WIDTH_Q : x * WIDTH_Q + NOPE]
        q_rope = q_ref[:, x * WIDTH_Q + NOPE : (x + 1) * WIDTH_Q]
        grad = g_ref[:, x * VDIM : (x + 1) * VDIM]
        for y in range(SIDE):
            slot = y * SIDE + x
            out_ref[slot, 0:ROWS] = key
            out_ref[slot, ROWS : 2 * ROWS] = value
            out_ref[slot, 2 * ROWS : KEY_ROWS] = rope
            first = slice(y * PIECE, (y + 1) * PIECE)
            second = slice(HALF + y * PIECE, HALF + (y + 1) * PIECE)
            low = KEY_ROWS
            out_ref[slot, low : low + PIECE] = q_nope[first]
            out_ref[slot, low + PIECE : low + 2 * PIECE] = q_nope[second]
            out_ref[slot, low + 2 * PIECE : low + 3 * PIECE] = grad[first]
            out_ref[slot, low + 3 * PIECE : low + 4 * PIECE] = grad[second]
            out_ref[slot, low + 4 * PIECE : low + 5 * PIECE] = jnp.concatenate(
                [q_rope[first], q_rope[second]], axis=1
            )


def attention_kernel(
    own_starts,
    other_starts,
    rank,
    group_chunks,
    qpos_ref,
    own_ref,
    other_ref,
    own_out,
    other_out,
    keys,
    values,
    queries,
    grads,
    scores,
    slopes,
    key_grads,
    value_grads,
    query_grads,
    key_sum,
    value_sum,
):
    pad = jnp.zeros((HALF, HALF), bf16)
    pad_piece = jnp.zeros((PIECE, HALF), bf16)

    def place(chip, carry):
        for starts, ref in ((own_starts, own_ref), (other_starts, other_ref)):
            rope = ref[chip, 2 * ROWS : KEY_ROWS]
            for half in range(2):
                at = pl.ds(pl.multiple_of(starts[2 * chip + half], HALF), HALF)
                keys[at, 0:NOPE] = ref[chip, half * HALF : (half + 1) * HALF]
                keys[at, NOPE : 2 * NOPE] = jnp.concatenate(
                    [rope[:, half * HALF : (half + 1) * HALF], pad], axis=1
                )
                values[at, :] = ref[chip, ROWS + half * HALF : ROWS + (half + 1) * HALF]
        low = KEY_ROWS
        q_rope = own_ref[chip, low + 4 * PIECE : low + 5 * PIECE]
        for half in range(2):
            at = pl.ds(pl.multiple_of(rank[2 * chip + half] * PIECE, PIECE), PIECE)
            queries[at, 0:NOPE] = own_ref[chip, low + half * PIECE : low + (half + 1) * PIECE]
            queries[at, NOPE : 2 * NOPE] = jnp.concatenate(
                [q_rope[:, half * HALF : (half + 1) * HALF], pad_piece], axis=1
            )
            grads[at, :] = own_ref[chip, low + (2 + half) * PIECE : low + (3 + half) * PIECE]
        return carry

    lax.fori_loop(0, CHIPS, place, 0)

    log_totals = []
    averages = []
    for group in range(N_GROUPS):
        lanes = slice(group * GROUP, (group + 1) * GROUP)
        q_group = queries[lanes, :]
        g_group = grads[lanes, :]
        q_pos = qpos_ref[0:1, lanes]

        def gather_stats(index, carry):
            top, weight_sum, weighted = carry
            at = pl.ds(pl.multiple_of(index * CHUNK, CHUNK), CHUNK)
            score = dot(keys[at, :], q_group, 1, 1) * (SCALE * LOG2E)
            k_pos = index * CHUNK + lax.broadcasted_iota(jnp.int32, (CHUNK, GROUP), 0)
            score = jnp.where(k_pos <= q_pos, score, masked_low)
            slope = dot(values[at, :], g_group, 1, 1)
            scores[at, lanes] = score
            slopes[at, lanes] = slope
            fresh = jnp.maximum(top, jnp.max(score, axis=0, keepdims=True))
            fade = jnp.exp2(top - fresh)
            weight = jnp.exp2(score - fresh)
            weight_sum = weight_sum * fade + jnp.sum(weight, axis=0, keepdims=True)
            weighted = weighted * fade + jnp.sum(weight * slope, axis=0, keepdims=True)
            return (fresh, weight_sum, weighted)

        zero = jnp.zeros((1, GROUP), f32)
        top, weight_sum, weighted = lax.fori_loop(
            0,
            group_chunks[group],
            gather_stats,
            (jnp.full((1, GROUP), masked_low, f32), zero, zero),
        )
        log_totals.append(top + jnp.log2(weight_sum))
        averages.append(weighted / weight_sum)

    query_grads[...] = jnp.zeros_like(query_grads)

    def gradients(index, carry):
        at = pl.ds(pl.multiple_of(index * CHUNK, CHUNK), CHUNK)
        key_sum[...] = jnp.zeros_like(key_sum)
        value_sum[...] = jnp.zeros_like(value_sum)
        for group in range(N_GROUPS):
            lanes = slice(group * GROUP, (group + 1) * GROUP)

            @pl.when(index < group_chunks[group])
            def _(lanes=lanes, group=group):
                probs = jnp.exp2(scores[at, lanes] - log_totals[group])
                score_grad = (probs * ((slopes[at, lanes] - averages[group]) * SCALE)).astype(bf16)
                value_sum[...] += dot(probs.astype(bf16), grads[lanes, :])
                key_sum[...] += dot(score_grad, queries[lanes, :])
                query_grads[lanes, :] += dot(score_grad, keys[at, :], 0, 0)

        key_grads[at, :] = key_sum[...].astype(bf16)
        value_grads[at, :] = value_sum[...].astype(bf16)
        return carry

    lax.fori_loop(0, N_CHUNKS, gradients, 0)

    def hand_out(chip, carry):
        low = KEY_ROWS
        for starts, ref in ((own_starts, own_out), (other_starts, other_out)):
            ropes = []
            for half in range(2):
                at = pl.ds(pl.multiple_of(starts[2 * chip + half], HALF), HALF)
                ref[chip, half * HALF : (half + 1) * HALF] = key_grads[at, 0:NOPE]
                ref[chip, ROWS + half * HALF : ROWS + (half + 1) * HALF] = value_grads[at, :]
                ropes.append(key_grads[at, NOPE:WIDTH_Q])
            ref[chip, 2 * ROWS : KEY_ROWS] = jnp.concatenate(ropes, axis=1)
        ropes = []
        for half in range(2):
            at = pl.ds(pl.multiple_of(rank[2 * chip + half] * PIECE, PIECE), PIECE)
            piece = query_grads[at, :].astype(bf16)
            own_out[chip, low + half * PIECE : low + (half + 1) * PIECE] = piece[:, 0:NOPE]
            ropes.append(piece[:, NOPE:WIDTH_Q])
        own_out[chip, low + 2 * PIECE : low + 3 * PIECE] = jnp.concatenate(ropes, axis=1)
        other_out[chip, low : low + 3 * PIECE] = jnp.zeros((3 * PIECE, NOPE), bf16)
        return carry

    lax.fori_loop(0, CHIPS, hand_out, 0)


def head_sums(slots_ref, low):
    parts = []
    for x in range(HEADS):
        total = slots_ref[x, low : low + ROWS].astype(f32)
        for y in range(1, SIDE):
            total = total + slots_ref[y * SIDE + x, low : low + ROWS].astype(f32)
        parts.append(total.astype(bf16))
    return jnp.concatenate(parts, axis=1)


def latent_kernel(slots_ref, wk_ref, wv_ref, out_ref):
    key_flat = head_sums(slots_ref, 0)
    value_flat = head_sums(slots_ref, ROWS)
    latent = dot(key_flat, wk_ref[...], 1, 1) + dot(value_flat, wv_ref[...], 1, 1)
    out_ref[:, :LATENT] = latent.astype(bf16)
    rope = slots_ref[0, 2 * ROWS : KEY_ROWS].astype(f32)
    for slot in range(1, CHIPS):
        rope = rope + slots_ref[slot, 2 * ROWS : KEY_ROWS].astype(f32)
    rope = jnp.concatenate([rope[:, :HALF], rope[:, HALF:]], axis=0)
    out_ref[:, LATENT:] = jnp.concatenate([rope, jnp.zeros_like(rope)], axis=1).astype(bf16)


def projection_kernel(core_ref, slots_ref, kv_ref, grad_q_ref, own_ref, other_ref, terms):
    normed = rms_rows(kv_ref[:, :LATENT])[0].astype(bf16)
    width = HEADS * NOPE
    terms[:, :width] = dot(normed, head_sums(slots_ref, 0), 0, 0).astype(bf16)
    terms[:, width:] = dot(normed, head_sums(slots_ref, ROWS), 0, 0).astype(bf16)
    rows = LATENT // (2 * CHIPS)
    core = core_ref[0]
    for chip in range(CHIPS):
        first = pl.multiple_of((2 * chip + core) * rows, rows)
        second = pl.multiple_of((2 * chip + 1 - core) * rows, rows)
        own_ref[chip] = terms[pl.ds(first, rows), :]
        other_ref[chip] = terms[pl.ds(second, rows), :]
    low = KEY_ROWS
    for y in range(SIDE):
        for half in range(2):
            parts = []
            for x in range(HEADS):
                slot = y * SIDE + x
                parts.append(slots_ref[slot, low + half * PIECE : low + (half + 1) * PIECE])
                rope = slots_ref[slot, low + 2 * PIECE : low + 3 * PIECE]
                parts.append(rope[:, half * HALF : (half + 1) * HALF])
            first = half * HALF + y * PIECE
            grad_q_ref[first : first + PIECE, :] = jnp.concatenate(parts, axis=1)


def norm_kernel(slots_ref, kv_ref, out_ref):
    total = jnp.sum(slots_ref[...].astype(f32), axis=0)
    x_hat, inverse = rms_rows(kv_ref[:, :LATENT])
    latent = total[:, :LATENT]
    latent = inverse * (latent - x_hat * jnp.mean(latent * x_hat, axis=-1, keepdims=True))
    row = jnp.concatenate([latent, total[:, LATENT:]], axis=1).astype(bf16)
    out_ref[...] = jnp.broadcast_to(row[None], out_ref.shape)


def call(kernel, shapes, specs, scratch=(), limit=32, flops=0, moved=0):
    shapes = [jax.ShapeDtypeStruct(*shape) for shape in shapes]
    single = len(shapes) == 1
    return pl.pallas_call(
        kernel,
        out_shape=shapes[0] if single else shapes,
        in_specs=specs,
        out_specs=VMEM if single else [VMEM] * len(shapes),
        scratch_shapes=scratch,
        compiler_params=pltpu.CompilerParams(vmem_limit_bytes=limit * 2**20),
        cost_estimate=pl.CostEstimate(flops=flops, bytes_accessed=moved, transcendentals=0),
    )


def local(query, kv_row, w_uk, w_uv, grad_out, block_start):
    ctx = lax.axis_index("ctx")
    chip, core = ctx // 2, ctx % 2
    z_size = lax.axis_size("head")
    z_rows = ROWS // z_size
    planes = [[2 * m + c for m in range(CHIPS)] for c in range(2)]
    swap = [(i, i ^ 1) for i in range(2 * CHIPS)]

    def over_chips(slots):
        return lax.all_to_all(slots, "ctx", 0, 0, axis_index_groups=planes)

    slots = call(expand_kernel, [((CHIPS, IN_ROWS, NOPE), bf16)], [VMEM] * 5)(
        kv_row, w_uk, w_uv, query, grad_out
    )
    own = over_chips(slots)
    other = lax.ppermute(own, "ctx", swap)

    starts = block_start.reshape(CHIPS, 2, 2)
    own_starts = lax.dynamic_index_in_dim(starts, core, 1, False).reshape(2 * CHIPS)
    other_starts = lax.dynamic_index_in_dim(starts, 1 - core, 1, False).reshape(2 * CHIPS)
    rank = jnp.sum((own_starts[None, :] < own_starts[:, None]).astype(jnp.int32), axis=1)
    places = jnp.arange(2 * CHIPS, dtype=jnp.int32)
    in_order = jnp.sum(jnp.where(rank[None, :] == places[:, None], own_starts[None, :], 0), axis=1)
    offset = (chip // SIDE) * PIECE
    q_pos = in_order[:, None] + offset + jnp.arange(PIECE, dtype=jnp.int32)[None, :]
    q_pos = jnp.broadcast_to(q_pos.reshape(1, QUERIES), (8, QUERIES))
    last = in_order.reshape(N_GROUPS, -1)[:, -1] + offset + PIECE - 1
    group_chunks = last // CHUNK + 1

    own_part, other_part = call(
        attention_kernel,
        [((CHIPS, OUT_ROWS, NOPE), bf16)] * 2,
        [SMEM] * 4 + [VMEM] * 3,
        [
            pltpu.VMEM((KEYS, 2 * NOPE), bf16),
            pltpu.VMEM((KEYS, VDIM), bf16),
            pltpu.VMEM((QUERIES, 2 * NOPE), bf16),
            pltpu.VMEM((QUERIES, VDIM), bf16),
            pltpu.VMEM((KEYS, QUERIES), f32),
            pltpu.VMEM((KEYS, QUERIES), f32),
            pltpu.VMEM((KEYS, 2 * NOPE), bf16),
            pltpu.VMEM((KEYS, VDIM), bf16),
            pltpu.VMEM((QUERIES, 2 * NOPE), f32),
            pltpu.VMEM((CHUNK, 2 * NOPE), f32),
            pltpu.VMEM((CHUNK, VDIM), f32),
        ],
        limit=48,
    )(own_starts, other_starts, rank, group_chunks, q_pos, own, other)
    summed = own_part + lax.ppermute(other_part, "ctx", swap)
    slots = over_chips(summed)

    z_part = call(latent_kernel, [((ROWS, Z_WIDTH), bf16)], [VMEM] * 3)(slots, w_uk, w_uv)
    z_part = z_part.reshape(z_size, z_rows, Z_WIDTH)
    z_slots = lax.all_to_all(z_part, "head", 0, 0)

    w_rows = LATENT // (2 * CHIPS)
    w_width = 2 * HEADS * NOPE
    grad_query, own_terms, other_terms = call(
        projection_kernel,
        [((ROWS, HEADS * WIDTH_Q), bf16)] + [((CHIPS, w_rows, w_width), bf16)] * 2,
        [SMEM] + [VMEM] * 2,
        [pltpu.VMEM((LATENT, w_width), bf16)],
        flops=2 * 128 * 512 * 1024,
        moved=8 * 2**20,
    )(core.reshape(1), slots, kv_row)
    own_terms = own_terms + lax.ppermute(other_terms, "ctx", swap)

    first_row = lax.axis_index("head") * z_rows
    kv_rows = lax.dynamic_slice_in_dim(kv_row, first_row, z_rows)
    rows = call(norm_kernel, [((z_size, z_rows, Z_WIDTH), bf16)], [VMEM] * 2)(z_slots, kv_rows)
    all_rows = lax.all_to_all(rows, "head", 0, 0).reshape(ROWS, Z_WIDTH)
    grad_kv_row = all_rows[:, : LATENT + ROPE].astype(f32)

    terms = jnp.sum(over_chips(own_terms).astype(f32), axis=0)
    half = HEADS * NOPE
    return (grad_query, grad_kv_row, terms[:, :half], terms[:, half:])


def solution(mesh):
    placed = (
        P("ctx", "head"),
        P("ctx", None),
        P(None, "head"),
        P(None, "head"),
        P("ctx", "head"),
        P(),
    )
    return jax.shard_map(
        local,
        mesh=mesh,
        in_specs=placed,
        out_specs=(P("ctx", "head"), P("ctx", None), P("ctx", "head"), P("ctx", "head")),
        check_vma=False,
    )
```

```python
import math

import jax
import jax.numpy as jnp
from jax import lax
from jax.experimental import pallas as pl
from jax.experimental.pallas import tpu as pltpu
from jax.sharding import Mesh
from jax.sharding import PartitionSpec as P

LATENT = 512
ROPE = 64
NOPE = 128
VDIM = 128
WIDTH_Q = NOPE + ROPE
HALF = 64
BLOCKS = 64
HEADS = 4
SIDE = 4
CHIPS = SIDE * SIDE
PIECE = HALF // 2
ROWS = 2 * HALF
KEYS = 2 * CHIPS * HALF
QUERIES = 2 * CHIPS * PIECE
KEY_ROWS = 2 * HALF + PIECE
IN_ROWS = KEY_ROWS + 5 * PIECE
OUT_ROWS = KEY_ROWS + 3 * PIECE
W_ROWS = LATENT // (2 * CHIPS)
W_WIDTH = HEADS * (NOPE + VDIM)
CHUNK = 512
GROUP = 512
N_CHUNKS = KEYS // CHUNK
N_GROUPS = QUERIES // GROUP
LISTED = 2 * CHIPS
KEY_RANK, QUERY_RANK, KEY_START, QUERY_START, SEEN = (i * LISTED for i in range(5))
SPARE = SEEN + N_GROUPS
META = SPARE + 8
Z_WIDTH = 640
LOG2E = 1.4426950408889634
SCALE = 1.0 / math.sqrt(WIDTH_Q)

eps = 1e-06
masked_low = -1e30
bf16 = jnp.bfloat16
f32 = jnp.float32
VMEM = pl.BlockSpec(memory_space=pltpu.VMEM)
SMEM = pl.BlockSpec(memory_space=pltpu.SMEM)
ANY = pl.BlockSpec(memory_space=pl.ANY)


def dot(left, right, left_dim=1, right_dim=0):
    return lax.dot_general(
        left, right, (((left_dim,), (right_dim,)), ((), ())), preferred_element_type=f32
    )


def rms_rows(latent):
    values = latent.astype(f32)
    inverse = lax.rsqrt(jnp.mean(values * values, axis=-1, keepdims=True) + eps)
    return (values * inverse, inverse)


def list_blocks(block_start, meta, holder):
    half = lax.axis_index("y") % 2
    core = lax.axis_index("core")

    def find(index, carry):
        holder[block_start[index] // HALF] = index
        return carry

    lax.fori_loop(0, BLOCKS, find, 0)

    def count(place, carry):
        n_keys, n_queries = carry
        index = holder[place]
        is_key = index % 2 == half
        is_query = (index // 2) % 2 == core
        meta[jnp.where(is_key, KEY_RANK + index // 2, SPARE)] = n_keys
        meta[jnp.where(is_key, KEY_START + n_keys, SPARE)] = place * HALF
        n_keys = n_keys + is_key.astype(jnp.int32)
        of_query = 2 * (index // 4) + index % 2
        meta[jnp.where(is_query, QUERY_RANK + of_query, SPARE)] = n_queries
        meta[jnp.where(is_query, QUERY_START + n_queries, SPARE)] = place * HALF
        meta[jnp.where(is_query, SEEN + n_queries // (GROUP // PIECE), SPARE)] = n_keys
        return (n_keys, n_queries + is_query.astype(jnp.int32))

    lax.fori_loop(0, BLOCKS, count, (0, 0))


def pack_kernel(
    block_start,
    kv_any,
    wk_any,
    wv_any,
    q_any,
    g_any,
    out_ref,
    meta,
    kv_ref,
    wk_ref,
    wv_ref,
    q_ref,
    g_ref,
    holder,
    sems,
):
    pairs = [(kv_any, kv_ref), (wk_any, wk_ref), (wv_any, wv_ref), (q_any, q_ref), (g_any, g_ref)]
    copies = [
        pltpu.make_async_copy(source, target, sems.at[index])
        for index, (source, target) in enumerate(pairs)
    ]
    for copy in copies:
        copy.start()
    list_blocks(block_start, meta, holder)
    for copy in copies:
        copy.wait()
    values = kv_ref[:LATENT, :].astype(f32)
    inverse = lax.rsqrt(jnp.mean(values * values, axis=0, keepdims=True) + eps)
    normed = (values * inverse).T.astype(bf16)
    rope = kv_ref[LATENT:, :].astype(f32).T.astype(bf16)
    keys = dot(normed, wk_ref[...]).astype(bf16)
    values = dot(normed, wv_ref[...]).astype(bf16)
    for x in range(HEADS):
        key = keys[:, x * NOPE : (x + 1) * NOPE]
        value = values[:, x * VDIM : (x + 1) * VDIM]
        q_nope = q_ref[:, x * WIDTH_Q : x * WIDTH_Q + NOPE]
        q_rope = q_ref[:, x * WIDTH_Q + NOPE : (x + 1) * WIDTH_Q]
        grad = g_ref[:, x * VDIM : (x + 1) * VDIM]
        for y in range(SIDE):
            slot = y * SIDE + x
            low = (y % 2) * HALF
            out_ref[slot, :HALF] = key[low : low + HALF]
            out_ref[slot, HALF : 2 * HALF] = value[low : low + HALF]
            out_ref[slot, 2 * HALF : KEY_ROWS] = jnp.concatenate(
                [rope[low : low + PIECE], rope[low + PIECE : low + HALF]], axis=1
            )
            first = slice((y // 2) * PIECE, (y // 2 + 1) * PIECE)
            second = slice(HALF + (y // 2) * PIECE, HALF + (y // 2 + 1) * PIECE)
            low = KEY_ROWS
            out_ref[slot, low : low + PIECE] = q_nope[first]
            out_ref[slot, low + PIECE : low + 2 * PIECE] = q_nope[second]
            out_ref[slot, low + 2 * PIECE : low + 3 * PIECE] = grad[first]
            out_ref[slot, low + 3 * PIECE : low + 4 * PIECE] = grad[second]
            out_ref[slot, low + 4 * PIECE : low + 5 * PIECE] = jnp.concatenate(
                [q_rope[first], q_rope[second]], axis=1
            )


def place_positions(meta, k_pos):
    rows = lax.broadcasted_iota(jnp.int32, (HALF, NOPE), 0)

    def body(rank, carry):
        at = pl.ds(pl.multiple_of(rank * HALF, HALF), HALF)
        k_pos[at, :] = rows + meta[KEY_START + rank]
        return carry

    lax.fori_loop(0, LISTED, body, 0)


def query_positions(meta, group):
    lane = lax.broadcasted_iota(jnp.int32, (1, GROUP), 1)
    count = GROUP // PIECE
    start = jnp.zeros((1, GROUP), jnp.int32)
    for piece in range(count):
        start = jnp.where(lane // PIECE == piece, meta[QUERY_START + group * count + piece], start)
    return start + (lax.axis_index("y") // 2) * PIECE + lane % PIECE


def seen_chunks(meta, group):
    return (meta[SEEN + group] * HALF + CHUNK - 1) // CHUNK


def stats_kernel(
    meta, own_ref, other_ref, keys, values, queries, grads, stats, k_pos
):
    core = lax.axis_index("core")
    pad_key = jnp.zeros((HALF, HALF), bf16)
    pad = jnp.zeros((PIECE, HALF), bf16)

    def place(chip, carry):
        for ref, side in ((own_ref, core), (other_ref, 1 - core)):
            rank = meta[KEY_RANK + 2 * chip + side]
            at = pl.ds(pl.multiple_of(rank * HALF, HALF), HALF)
            rope = ref[chip, 2 * HALF : KEY_ROWS]
            rope = jnp.concatenate([rope[:, :HALF], rope[:, HALF:]], axis=0)
            keys[at, :NOPE] = ref[chip, :HALF]
            keys[at, NOPE:] = jnp.concatenate([rope, pad_key], axis=1)
            values[at, :] = ref[chip, HALF : 2 * HALF]
        low = KEY_ROWS
        q_rope = own_ref[chip, low + 4 * PIECE : low + 5 * PIECE]
        for half in range(2):
            rank = meta[QUERY_RANK + 2 * chip + half]
            at = pl.ds(pl.multiple_of(rank * PIECE, PIECE), PIECE)
            queries[at, :NOPE] = own_ref[chip, low + half * PIECE : low + (half + 1) * PIECE]
            queries[at, NOPE:] = jnp.concatenate(
                [q_rope[:, half * HALF : (half + 1) * HALF], pad], axis=1
            )
            grads[at, :] = own_ref[chip, low + (2 + half) * PIECE : low + (3 + half) * PIECE]
        return carry

    lax.fori_loop(0, CHIPS, place, 0)
    place_positions(meta, k_pos)

    for group in range(N_GROUPS):
        lanes = slice(group * GROUP, (group + 1) * GROUP)
        q_group = queries[lanes, :]
        g_group = grads[lanes, :]
        q_pos = query_positions(meta, group)

        def gather_stats(index, carry):
            top, weight_sum, weighted = carry
            at = pl.ds(pl.multiple_of(index * CHUNK, CHUNK), CHUNK)
            score = dot(keys[at, :], q_group, 1, 1) * (SCALE * LOG2E)
            key_at = jnp.concatenate([k_pos[at, :]] * (GROUP // NOPE), axis=1)
            score = jnp.where(key_at <= q_pos, score, masked_low)
            slope = dot(values[at, :], g_group, 1, 1)
            fresh = jnp.maximum(top, jnp.max(score, axis=0, keepdims=True))
            fade = jnp.exp2(top - fresh)
            weight = jnp.exp2(score - fresh)
            weight_sum = weight_sum * fade + jnp.sum(weight, axis=0, keepdims=True)
            weighted = weighted * fade + jnp.sum(weight * slope, axis=0, keepdims=True)
            return (fresh, weight_sum, weighted)

        zero = jnp.zeros((1, GROUP), f32)
        top, weight_sum, weighted = lax.fori_loop(
            0,
            seen_chunks(meta, group),
            gather_stats,
            (jnp.full((1, GROUP), masked_low, f32), zero, zero),
        )
        stats[:, lanes] = jnp.concatenate(
            [top, weight_sum, weighted, jnp.zeros((5, GROUP), f32)], axis=0
        )


def gradient_kernel(
    meta,
    keys,
    values,
    queries,
    grads,
    own_stats,
    other_stats,
    own_out,
    other_out,
    k_pos,
    key_grads,
    value_grads,
    query_grads,
    key_sum,
    value_sum,
):
    place_positions(meta, k_pos)
    own_top = own_stats[0:1, :]
    other_top = other_stats[0:1, :]
    top = jnp.maximum(own_top, other_top)
    own_fade = jnp.exp2(own_top - top)
    other_fade = jnp.exp2(other_top - top)
    weight_sum = own_stats[1:2, :] * own_fade + other_stats[1:2, :] * other_fade
    weighted = own_stats[2:3, :] * own_fade + other_stats[2:3, :] * other_fade
    log_total = top + jnp.log2(weight_sum)
    average = weighted / weight_sum
    query_grads[...] = jnp.zeros_like(query_grads)
    positions = [query_positions(meta, group) for group in range(N_GROUPS)]

    def gradients(index, carry):
        at = pl.ds(pl.multiple_of(index * CHUNK, CHUNK), CHUNK)
        key_sum[...] = jnp.zeros_like(key_sum)
        value_sum[...] = jnp.zeros_like(value_sum)
        for group in range(N_GROUPS):
            lanes = slice(group * GROUP, (group + 1) * GROUP)

            @pl.when(index < seen_chunks(meta, group))
            def _(lanes=lanes, q_pos=positions[group]):
                score = dot(keys[at, :], queries[lanes, :], 1, 1) * (SCALE * LOG2E)
                key_at = jnp.concatenate([k_pos[at, :]] * (GROUP // NOPE), axis=1)
                score = jnp.where(key_at <= q_pos, score - log_total[:, lanes], masked_low)
                slope = dot(values[at, :], grads[lanes, :], 1, 1)
                probs = jnp.exp2(score)
                score_grad = (probs * ((slope - average[:, lanes]) * SCALE)).astype(bf16)
                value_sum[...] += dot(probs.astype(bf16), grads[lanes, :])
                key_sum[...] += dot(score_grad, queries[lanes, :])
                query_grads[lanes, :] += dot(score_grad, keys[at, :], 0, 0)

        key_grads[at, :] = key_sum[...].astype(bf16)
        value_grads[at, :] = value_sum[...].astype(bf16)
        return carry

    lax.fori_loop(0, N_CHUNKS, gradients, 0)
    core = lax.axis_index("core")

    def hand_out(chip, carry):
        for ref, side in ((own_out, core), (other_out, 1 - core)):
            rank = meta[KEY_RANK + 2 * chip + side]
            at = pl.ds(pl.multiple_of(rank * HALF, HALF), HALF)
            ref[chip, :HALF] = key_grads[at, :NOPE]
            ref[chip, HALF : 2 * HALF] = value_grads[at, :]
            rope = key_grads[at, NOPE:WIDTH_Q]
            ref[chip, 2 * HALF : KEY_ROWS] = jnp.concatenate([rope[:PIECE], rope[PIECE:]], axis=1)
        low = KEY_ROWS
        ropes = []
        for half in range(2):
            rank = meta[QUERY_RANK + 2 * chip + half]
            at = pl.ds(pl.multiple_of(rank * PIECE, PIECE), PIECE)
            piece = query_grads[at, :].astype(bf16)
            own_out[chip, low + half * PIECE : low + (half + 1) * PIECE] = piece[:, :NOPE]
            ropes.append(piece[:, NOPE:WIDTH_Q])
        own_out[chip, low + 2 * PIECE : low + 3 * PIECE] = jnp.concatenate(ropes, axis=1)
        return carry

    lax.fori_loop(0, CHIPS, hand_out, 0)


def slot_sum(slots_ref, slots, low, rows):
    total = slots_ref[slots[0], low : low + rows].astype(f32)
    for slot in slots[1:]:
        total = total + slots_ref[slot, low : low + rows].astype(f32)
    return total


def head_sums(slots_ref, low):
    parts = []
    for x in range(HEADS):
        halves = [
            slot_sum(slots_ref, (y * SIDE + x, (y + 2) * SIDE + x), low, HALF) for y in range(2)
        ]
        parts.append(jnp.concatenate(halves, axis=0).astype(bf16))
    return jnp.concatenate(parts, axis=1)


def latent_kernel(slots_ref, wk_ref, wv_ref, out_ref):
    key_flat = head_sums(slots_ref, 0)
    value_flat = head_sums(slots_ref, HALF)
    latent = dot(key_flat, wk_ref[...], 1, 1) + dot(value_flat, wv_ref[...], 1, 1)
    out_ref[:, :LATENT] = latent.astype(bf16)
    ropes = []
    for y in range(2):
        slots = [row * SIDE + x for row in (y, y + 2) for x in range(HEADS)]
        rope = slot_sum(slots_ref, slots, 2 * HALF, PIECE)
        ropes += [rope[:, :HALF], rope[:, HALF:]]
    rope = jnp.concatenate(ropes, axis=0)
    out_ref[:, LATENT:] = jnp.concatenate([rope, jnp.zeros_like(rope)], axis=1).astype(bf16)


def projection_kernel(slots_ref, kv_ref, grad_q_ref, own_ref, other_ref, terms):
    values = kv_ref[:LATENT, :].astype(f32)
    inverse = lax.rsqrt(jnp.mean(values * values, axis=0, keepdims=True) + eps)
    normed = (values * inverse).astype(bf16)
    terms[:, : HEADS * NOPE] = dot(normed, head_sums(slots_ref, 0)).astype(bf16)
    terms[:, HEADS * NOPE :] = dot(normed, head_sums(slots_ref, HALF)).astype(bf16)
    core = lax.axis_index("core")
    y_here, x_here = lax.axis_index("y"), lax.axis_index("x")
    for dx in range(SIDE):
        for dy in range(SIDE):
            chip = (y_here ^ dy) * SIDE + (x_here ^ dx)
            first = pl.multiple_of((2 * chip + core) * W_ROWS, W_ROWS)
            second = pl.multiple_of((2 * chip + 1 - core) * W_ROWS, W_ROWS)
            own_ref[dx, dy] = terms[pl.ds(first, W_ROWS), :]
            other_ref[dx, dy] = terms[pl.ds(second, W_ROWS), :]
    low = KEY_ROWS
    for quarter in range(2):
        for half in range(2):
            parts = []
            for x in range(HEADS):
                slots = (2 * quarter * SIDE + x, (2 * quarter + 1) * SIDE + x)
                parts.append(slot_sum(slots_ref, slots, low + half * PIECE, PIECE))
                rope = slot_sum(slots_ref, slots, low + 2 * PIECE, PIECE)
                parts.append(rope[:, half * HALF : (half + 1) * HALF])
            first = half * HALF + quarter * PIECE
            grad_q_ref[first : first + PIECE, :] = jnp.concatenate(parts, axis=1).astype(bf16)


def norm_kernel(slots_ref, kv_ref, out_ref):
    total = jnp.sum(slots_ref[...].astype(f32), axis=0)
    x_hat, inverse = rms_rows(kv_ref[:, :LATENT])
    latent = total[:, :LATENT]
    latent = inverse * (latent - x_hat * jnp.mean(latent * x_hat, axis=-1, keepdims=True))
    row = jnp.concatenate([latent, total[:, LATENT:]], axis=1).astype(bf16)
    out_ref[...] = jnp.broadcast_to(row[None], out_ref.shape)


def call(kernel, shapes, specs, scratch=(), limit=32, flops=0, moved=0, out_specs=None):
    shapes = [jax.ShapeDtypeStruct(*shape) for shape in shapes]
    single = len(shapes) == 1
    if out_specs is None:
        out_specs = VMEM if single else [VMEM] * len(shapes)
    return pl.pallas_call(
        kernel,
        out_shape=shapes[0] if single else shapes,
        in_specs=specs,
        out_specs=out_specs,
        scratch_shapes=scratch,
        compiler_params=pltpu.CompilerParams(vmem_limit_bytes=limit * 2**20),
        cost_estimate=pl.CostEstimate(flops=flops, bytes_accessed=moved, transcendentals=0),
    )


def over_chips(slots):
    return lax.all_to_all(slots, ("y", "x"), 0, 0)


def swap(array, axis, bit):
    return lax.ppermute(array, axis, [(i, i ^ bit) for i in range(lax.axis_size(axis))])


def local(query, kv_row, w_uk, w_uv, grad_out, block_start):
    z_size = lax.axis_size("head")
    z_rows = ROWS // z_size
    kv_t = kv_row.T
    slots, meta = call(
        pack_kernel,
        [((CHIPS, IN_ROWS, NOPE), bf16), ((META,), jnp.int32)],
        [SMEM] + [ANY] * 5,
        [
            pltpu.VMEM((LATENT + ROPE, ROWS), bf16),
            pltpu.VMEM((LATENT, HEADS * NOPE), bf16),
            pltpu.VMEM((LATENT, HEADS * VDIM), bf16),
            pltpu.VMEM((ROWS, HEADS * WIDTH_Q), bf16),
            pltpu.VMEM((ROWS, HEADS * VDIM), bf16),
            pltpu.SMEM((BLOCKS,), jnp.int32),
            pltpu.SemaphoreType.DMA((5,)),
        ],
        limit=60,
        out_specs=[VMEM, SMEM],
    )(block_start, kv_t, w_uk, w_uv, query, grad_out)
    own = over_chips(slots)
    other = swap(own[:, :KEY_ROWS], "core", 1)

    keys, values, queries, grads, stats = call(
        stats_kernel,
        [
            ((KEYS, 2 * NOPE), bf16),
            ((KEYS, VDIM), bf16),
            ((QUERIES, 2 * NOPE), bf16),
            ((QUERIES, VDIM), bf16),
            ((8, QUERIES), f32),
        ],
        [SMEM] + [VMEM] * 2,
        [pltpu.VMEM((KEYS, NOPE), jnp.int32)],
    )(meta, own, other)
    own_part, other_part = call(
        gradient_kernel,
        [((CHIPS, OUT_ROWS, NOPE), bf16), ((CHIPS, KEY_ROWS, NOPE), bf16)],
        [SMEM] + [VMEM] * 6,
        [
            pltpu.VMEM((KEYS, NOPE), jnp.int32),
            pltpu.VMEM((KEYS, 2 * NOPE), bf16),
            pltpu.VMEM((KEYS, VDIM), bf16),
            pltpu.VMEM((QUERIES, 2 * NOPE), f32),
            pltpu.VMEM((CHUNK, 2 * NOPE), f32),
            pltpu.VMEM((CHUNK, VDIM), f32),
        ],
    )(meta, keys, values, queries, grads, stats, swap(stats, "y", 1))
    slots = over_chips(own_part.at[:, :KEY_ROWS].add(swap(other_part, "core", 1)))

    z_part = call(latent_kernel, [((ROWS, Z_WIDTH), bf16)], [VMEM] * 3)(slots, w_uk, w_uv)
    z_slots = lax.all_to_all(z_part.reshape(z_size, z_rows, Z_WIDTH), "head", 0, 0)

    grad_query, own_terms, other_terms = call(
        projection_kernel,
        [((ROWS, HEADS * WIDTH_Q), bf16)] + [((SIDE, SIDE, W_ROWS, W_WIDTH), bf16)] * 2,
        [VMEM] * 2,
        [pltpu.VMEM((LATENT, W_WIDTH), bf16)],
        flops=2 * ROWS * LATENT * W_WIDTH,
        moved=8 * 2**20,
    )(slots, kv_t)
    terms = own_terms + swap(other_terms, "core", 1)
    for axis in ("x", "y"):
        total = terms[0].astype(f32)
        for bit in range(1, SIDE):
            total = total + swap(terms[bit], axis, bit).astype(f32)
        terms = total.astype(bf16)

    first_row = lax.axis_index("head") * z_rows
    kv_rows = lax.dynamic_slice_in_dim(kv_row, first_row, z_rows)
    rows = call(norm_kernel, [((z_size, z_rows, Z_WIDTH), bf16)], [VMEM] * 2)(z_slots, kv_rows)
    all_rows = lax.all_to_all(rows, "head", 0, 0).reshape(ROWS, Z_WIDTH)
    grad_kv_row = all_rows[:, : LATENT + ROPE].astype(f32)
    width = HEADS * NOPE
    return (grad_query, grad_kv_row, total[:, :width], total[:, width:])


def solution(mesh):
    axes = ("y", "x", "core")
    devices = mesh.devices.reshape(SIDE, SIDE, 2, mesh.shape["head"])
    placed = (
        P(axes, "head"),
        P(axes, None),
        P(None, "head"),
        P(None, "head"),
        P(axes, "head"),
        P(),
    )
    return jax.shard_map(
        local,
        mesh=Mesh(devices, (*axes, "head")),
        in_specs=placed,
        out_specs=(P(axes, "head"), P(axes, None), P(axes, "head"), P(axes, "head")),
        check_vma=False,
    )
```

```python
import math

import jax
import jax.numpy as jnp
from jax import lax
from jax.experimental import pallas as pl
from jax.experimental.pallas import tpu as pltpu
from jax.sharding import Mesh
from jax.sharding import PartitionSpec as P

LATENT = 512
ROPE = 64
NOPE = 128
VDIM = 128
WIDTH_Q = NOPE + ROPE
HALF = 64
BLOCKS = 64
HEADS = 4
SIDE = 4
CHIPS = SIDE * SIDE
PIECE = HALF // 2
ROWS = 2 * HALF
KEYS = 2 * CHIPS * HALF
QUERIES = 2 * CHIPS * PIECE
KEY_ROWS = 2 * HALF + PIECE
IN_ROWS = KEY_ROWS + 5 * PIECE
OUT_ROWS = KEY_ROWS + 3 * PIECE
W_ROWS = LATENT // (2 * CHIPS)
W_WIDTH = HEADS * (NOPE + VDIM)
CHUNK = 1024
GROUP = 512
N_CHUNKS = KEYS // CHUNK
N_GROUPS = QUERIES // GROUP
UNROLL = CHIPS
Z_WIDTH = 640
LOG2E = 1.4426950408889634
SCALE = 1.0 / math.sqrt(WIDTH_Q)

eps = 1e-06
masked_low = -1e30
bf16 = jnp.bfloat16
f32 = jnp.float32
VMEM = pl.BlockSpec(memory_space=pltpu.VMEM)
SMEM = pl.BlockSpec(memory_space=pltpu.SMEM)
ANY = pl.BlockSpec(memory_space=pl.ANY)


def dot(left, right, left_dim=1, right_dim=0):
    return lax.dot_general(
        left, right, (((left_dim,), (right_dim,)), ((), ())), preferred_element_type=f32
    )


def rms_rows(latent):
    values = latent.astype(f32)
    inverse = lax.rsqrt(jnp.mean(values * values, axis=-1, keepdims=True) + eps)
    return (values * inverse, inverse)


def list_blocks(starts, meta, q_pos):
    half = lax.axis_index("y") % 2
    core = lax.axis_index("core")
    shape = (BLOCKS, BLOCKS)
    across = jnp.broadcast_to(starts[...], shape)
    down = across.T
    row = lax.broadcasted_iota(jnp.int32, shape, 0)
    lane = lax.broadcasted_iota(jnp.int32, shape, 1)

    def tally(where, axis):
        return jnp.sum(where.astype(jnp.int32), axis=axis, keepdims=True)

    key_rank = tally((down < across) & (row % 2 == half), 0)
    query_rank = tally((down < across) & ((row // 2) % 2 == core), 0)
    query_rank_down = tally((across < down) & ((lane // 2) % 2 == core), 1)
    is_query = (row[:, :1] // 2) % 2 == core
    shape = (BLOCKS, QUERIES)
    piece = lax.broadcasted_iota(jnp.int32, shape, 1) // PIECE
    mine = (query_rank_down == piece) & is_query
    position = jnp.sum(jnp.where(mine, down[:, :1], 0), axis=0, keepdims=True)
    seen = []
    for group in range(N_GROUPS):
        last = position[:, (group + 1) * GROUP - 1 : (group + 1) * GROUP]
        seen.append(tally((across[:1] <= last) & (lane[:1] % 2 == half), 1))
    seen = jnp.concatenate(seen + [jnp.zeros((1, BLOCKS - N_GROUPS), jnp.int32)], axis=1)
    rest = jnp.zeros((5, BLOCKS), jnp.int32)
    meta[...] = jnp.concatenate([key_rank, query_rank, seen, rest], axis=0)
    offset = lax.broadcasted_iota(jnp.int32, (1, QUERIES), 1) % PIECE
    offset = offset + (lax.axis_index("y") // 2) * PIECE
    q_pos[...] = jnp.broadcast_to(position + offset, q_pos.shape)


def pack_kernel(
    block_start,
    kv_any,
    wk_any,
    wv_any,
    q_any,
    g_any,
    out_any,
    meta,
    q_pos,
    kv_ref,
    wk_ref,
    wv_ref,
    q_ref,
    g_ref,
    out_ref,
    sems,
    out_sems,
):
    pairs = [(q_any, q_ref), (g_any, g_ref), (kv_any, kv_ref), (wk_any, wk_ref), (wv_any, wv_ref)]
    copies = [
        pltpu.make_async_copy(source, target, sems.at[index])
        for index, (source, target) in enumerate(pairs)
    ]
    for copy in copies:
        copy.start()
    list_blocks(block_start, meta, q_pos)
    copies[0].wait()
    copies[1].wait()
    for x in range(HEADS):
        q_nope = q_ref[:, x * WIDTH_Q : x * WIDTH_Q + NOPE]
        q_rope = q_ref[:, x * WIDTH_Q + NOPE : (x + 1) * WIDTH_Q]
        grad = g_ref[:, x * VDIM : (x + 1) * VDIM]
        for y in range(SIDE):
            slot = y * SIDE + x
            first = slice((y // 2) * PIECE, (y // 2 + 1) * PIECE)
            second = slice(HALF + (y // 2) * PIECE, HALF + (y // 2 + 1) * PIECE)
            low = KEY_ROWS
            out_ref[slot, low : low + PIECE] = q_nope[first]
            out_ref[slot, low + PIECE : low + 2 * PIECE] = q_nope[second]
            out_ref[slot, low + 2 * PIECE : low + 3 * PIECE] = grad[first]
            out_ref[slot, low + 3 * PIECE : low + 4 * PIECE] = grad[second]
            out_ref[slot, low + 4 * PIECE : low + 5 * PIECE] = jnp.concatenate(
                [q_rope[first], q_rope[second]], axis=1
            )
    copies[2].wait()
    values = kv_ref[:LATENT, :].astype(f32)
    inverse = lax.rsqrt(jnp.mean(values * values, axis=0, keepdims=True) + eps)
    normed = (values * inverse).T.astype(bf16)
    rope = kv_ref[LATENT:, :].astype(f32).T.astype(bf16)
    copies[3].wait()
    keys = dot(normed, wk_ref[...]).astype(bf16)
    copies[4].wait()
    values = dot(normed, wv_ref[...]).astype(bf16)
    sent = []
    for y in range(SIDE):
        low = (y % 2) * HALF
        for x in range(HEADS):
            slot = y * SIDE + x
            out_ref[slot, :HALF] = keys[low : low + HALF, x * NOPE : (x + 1) * NOPE]
            out_ref[slot, HALF : 2 * HALF] = values[low : low + HALF, x * VDIM : (x + 1) * VDIM]
            out_ref[slot, 2 * HALF : KEY_ROWS] = jnp.concatenate(
                [rope[low : low + PIECE], rope[low + PIECE : low + HALF]], axis=1
            )
        part = pl.ds(y * SIDE, SIDE)
        sent.append(pltpu.make_async_copy(out_ref.at[part], out_any.at[part], out_sems.at[y]))
        sent[-1].start()
    for copy in sent:
        copy.wait()


def key_block(chip, core):
    return (2 * chip + core) * 2 + lax.axis_index("y") % 2


def place_positions(block_start, meta, k_pos):
    rows = lax.broadcasted_iota(jnp.int32, (HALF, NOPE), 0)

    def body(index, carry):
        block = 2 * index + lax.axis_index("y") % 2
        at = pl.ds(pl.multiple_of(meta[0, block] * HALF, HALF), HALF)
        k_pos[at, :] = rows + block_start[block]
        return carry

    lax.fori_loop(0, 2 * CHIPS, body, 0, unroll=UNROLL)


def seen_chunks(meta, group):
    return (meta[2, group] * HALF + CHUNK - 1) // CHUNK


def stats_kernel(
    block_start, meta, q_pos, own_ref, other_ref, keys, values, queries, grads, stats, k_pos
):
    core = lax.axis_index("core")
    pad_key = jnp.zeros((HALF, HALF), bf16)
    pad = jnp.zeros((PIECE, HALF), bf16)

    def place(chip, carry):
        for ref, side in ((own_ref, core), (other_ref, 1 - core)):
            rank = meta[0, key_block(chip, side)]
            at = pl.ds(pl.multiple_of(rank * HALF, HALF), HALF)
            rope = ref[chip, 2 * HALF : KEY_ROWS]
            rope = jnp.concatenate([rope[:, :HALF], rope[:, HALF:]], axis=0)
            keys[at, :NOPE] = ref[chip, :HALF]
            keys[at, NOPE:] = jnp.concatenate([rope, pad_key], axis=1)
            values[at, :] = ref[chip, HALF : 2 * HALF]
        low = KEY_ROWS
        q_rope = own_ref[chip, low + 4 * PIECE : low + 5 * PIECE]
        for half in range(2):
            rank = meta[1, (2 * chip + core) * 2 + half]
            at = pl.ds(pl.multiple_of(rank * PIECE, PIECE), PIECE)
            queries[at, :NOPE] = own_ref[chip, low + half * PIECE : low + (half + 1) * PIECE]
            queries[at, NOPE:] = jnp.concatenate(
                [q_rope[:, half * HALF : (half + 1) * HALF], pad], axis=1
            )
            grads[at, :] = own_ref[chip, low + (2 + half) * PIECE : low + (3 + half) * PIECE]
        return carry

    lax.fori_loop(0, CHIPS, place, 0, unroll=UNROLL)
    place_positions(block_start, meta, k_pos)

    for group in range(N_GROUPS):
        lanes = slice(group * GROUP, (group + 1) * GROUP)
        q_group = queries[lanes, :]
        g_group = grads[lanes, :]
        q_at = q_pos[0:1, lanes]

        def gather_stats(index, carry):
            top, weight_sum, weighted = carry
            at = pl.ds(pl.multiple_of(index * CHUNK, CHUNK), CHUNK)
            score = dot(keys[at, :], q_group, 1, 1) * (SCALE * LOG2E)
            key_at = jnp.concatenate([k_pos[at, :]] * (GROUP // NOPE), axis=1)
            score = jnp.where(key_at <= q_at, score, masked_low)
            slope = dot(values[at, :], g_group, 1, 1)
            fresh = jnp.maximum(top, jnp.max(score, axis=0, keepdims=True))
            fade = jnp.exp2(top - fresh)
            weight = jnp.exp2(score - fresh)
            weight_sum = weight_sum * fade + jnp.sum(weight, axis=0, keepdims=True)
            weighted = weighted * fade + jnp.sum(weight * slope, axis=0, keepdims=True)
            return (fresh, weight_sum, weighted)

        zero = jnp.zeros((1, GROUP), f32)
        top, weight_sum, weighted = lax.fori_loop(
            0,
            seen_chunks(meta, group),
            gather_stats,
            (jnp.full((1, GROUP), masked_low, f32), zero, zero),
        )
        stats[:, lanes] = jnp.concatenate(
            [top, weight_sum, weighted, jnp.zeros((5, GROUP), f32)], axis=0
        )


def gradient_kernel(
    block_start,
    meta,
    q_pos,
    keys,
    values,
    queries,
    grads,
    own_stats,
    other_stats,
    own_out,
    other_out,
    k_pos,
    key_grads,
    value_grads,
    query_grads,
    key_sum,
    value_sum,
):
    place_positions(block_start, meta, k_pos)
    own_top = own_stats[0:1, :]
    other_top = other_stats[0:1, :]
    top = jnp.maximum(own_top, other_top)
    own_fade = jnp.exp2(own_top - top)
    other_fade = jnp.exp2(other_top - top)
    weight_sum = own_stats[1:2, :] * own_fade + other_stats[1:2, :] * other_fade
    weighted = own_stats[2:3, :] * own_fade + other_stats[2:3, :] * other_fade
    log_total = top + jnp.log2(weight_sum)
    average = weighted / weight_sum
    query_grads[...] = jnp.zeros_like(query_grads)

    def gradients(index, carry):
        at = pl.ds(pl.multiple_of(index * CHUNK, CHUNK), CHUNK)
        key_sum[...] = jnp.zeros_like(key_sum)
        value_sum[...] = jnp.zeros_like(value_sum)
        for group in range(N_GROUPS):
            lanes = slice(group * GROUP, (group + 1) * GROUP)

            @pl.when(index < seen_chunks(meta, group))
            def _(lanes=lanes):
                score = dot(keys[at, :], queries[lanes, :], 1, 1) * (SCALE * LOG2E)
                key_at = jnp.concatenate([k_pos[at, :]] * (GROUP // NOPE), axis=1)
                visible = key_at <= q_pos[0:1, lanes]
                score = jnp.where(visible, score - log_total[:, lanes], masked_low)
                slope = dot(values[at, :], grads[lanes, :], 1, 1)
                probs = jnp.exp2(score)
                score_grad = (probs * ((slope - average[:, lanes]) * SCALE)).astype(bf16)
                value_sum[...] += dot(probs.astype(bf16), grads[lanes, :])
                key_sum[...] += dot(score_grad, queries[lanes, :])
                query_grads[lanes, :] += dot(score_grad, keys[at, :], 0, 0)

        key_grads[at, :] = key_sum[...].astype(bf16)
        value_grads[at, :] = value_sum[...].astype(bf16)
        return carry

    lax.fori_loop(0, N_CHUNKS, gradients, 0)
    core = lax.axis_index("core")

    def hand_out(chip, carry):
        for ref, side in ((own_out, core), (other_out, 1 - core)):
            rank = meta[0, key_block(chip, side)]
            at = pl.ds(pl.multiple_of(rank * HALF, HALF), HALF)
            ref[chip, :HALF] = key_grads[at, :NOPE]
            ref[chip, HALF : 2 * HALF] = value_grads[at, :]
            rope = key_grads[at, NOPE:WIDTH_Q]
            ref[chip, 2 * HALF : KEY_ROWS] = jnp.concatenate([rope[:PIECE], rope[PIECE:]], axis=1)
        low = KEY_ROWS
        ropes = []
        for half in range(2):
            rank = meta[1, (2 * chip + core) * 2 + half]
            at = pl.ds(pl.multiple_of(rank * PIECE, PIECE), PIECE)
            piece = query_grads[at, :].astype(bf16)
            own_out[chip, low + half * PIECE : low + (half + 1) * PIECE] = piece[:, :NOPE]
            ropes.append(piece[:, NOPE:WIDTH_Q])
        own_out[chip, low + 2 * PIECE : low + 3 * PIECE] = jnp.concatenate(ropes, axis=1)
        return carry

    lax.fori_loop(0, CHIPS, hand_out, 0, unroll=UNROLL)


def slot_sum(slots_ref, slots, low, rows):
    total = slots_ref[slots[0], low : low + rows].astype(f32)
    for slot in slots[1:]:
        total = total + slots_ref[slot, low : low + rows].astype(f32)
    return total


def head_sums(slots_ref, low):
    parts = []
    for x in range(HEADS):
        halves = [
            slot_sum(slots_ref, (y * SIDE + x, (y + 2) * SIDE + x), low, HALF) for y in range(2)
        ]
        parts.append(jnp.concatenate(halves, axis=0).astype(bf16))
    return jnp.concatenate(parts, axis=1)


def latent_kernel(slots_ref, wk_ref, wv_ref, out_ref):
    key_flat = head_sums(slots_ref, 0)
    value_flat = head_sums(slots_ref, HALF)
    latent = dot(key_flat, wk_ref[...], 1, 1) + dot(value_flat, wv_ref[...], 1, 1)
    out_ref[:, :LATENT] = latent.astype(bf16)
    ropes = []
    for y in range(2):
        slots = [row * SIDE + x for row in (y, y + 2) for x in range(HEADS)]
        rope = slot_sum(slots_ref, slots, 2 * HALF, PIECE)
        ropes += [rope[:, :HALF], rope[:, HALF:]]
    rope = jnp.concatenate(ropes, axis=0)
    out_ref[:, LATENT:] = jnp.concatenate([rope, jnp.zeros_like(rope)], axis=1).astype(bf16)


def projection_kernel(slots_ref, kv_ref, grad_q_ref, own_ref, other_ref, terms):
    values = kv_ref[:LATENT, :].astype(f32)
    inverse = lax.rsqrt(jnp.mean(values * values, axis=0, keepdims=True) + eps)
    normed = (values * inverse).astype(bf16)
    terms[:, : HEADS * NOPE] = dot(normed, head_sums(slots_ref, 0)).astype(bf16)
    terms[:, HEADS * NOPE :] = dot(normed, head_sums(slots_ref, HALF)).astype(bf16)
    core = lax.axis_index("core")
    y_here, x_here = lax.axis_index("y"), lax.axis_index("x")
    for dx in range(SIDE):
        for dy in range(SIDE):
            chip = (y_here ^ dy) * SIDE + (x_here ^ dx)
            first = pl.multiple_of((2 * chip + core) * W_ROWS, W_ROWS)
            second = pl.multiple_of((2 * chip + 1 - core) * W_ROWS, W_ROWS)
            own_ref[dx, dy] = terms[pl.ds(first, W_ROWS), :]
            other_ref[dx, dy] = terms[pl.ds(second, W_ROWS), :]
    low = KEY_ROWS
    for quarter in range(2):
        for half in range(2):
            parts = []
            for x in range(HEADS):
                slots = (2 * quarter * SIDE + x, (2 * quarter + 1) * SIDE + x)
                parts.append(slot_sum(slots_ref, slots, low + half * PIECE, PIECE))
                rope = slot_sum(slots_ref, slots, low + 2 * PIECE, PIECE)
                parts.append(rope[:, half * HALF : (half + 1) * HALF])
            first = half * HALF + quarter * PIECE
            grad_q_ref[first : first + PIECE, :] = jnp.concatenate(parts, axis=1).astype(bf16)


def norm_kernel(slots_ref, kv_ref, out_ref):
    total = jnp.sum(slots_ref[...].astype(f32), axis=0)
    x_hat, inverse = rms_rows(kv_ref[:, :LATENT])
    latent = total[:, :LATENT]
    latent = inverse * (latent - x_hat * jnp.mean(latent * x_hat, axis=-1, keepdims=True))
    row = jnp.concatenate([latent, total[:, LATENT:]], axis=1).astype(bf16)
    out_ref[...] = jnp.broadcast_to(row[None], out_ref.shape)


def call(kernel, shapes, specs, scratch=(), limit=32, flops=0, moved=0, out_specs=None):
    shapes = [jax.ShapeDtypeStruct(*shape) for shape in shapes]
    single = len(shapes) == 1
    if out_specs is None:
        out_specs = VMEM if single else [VMEM] * len(shapes)
    return pl.pallas_call(
        kernel,
        out_shape=shapes[0] if single else shapes,
        in_specs=specs,
        out_specs=out_specs,
        scratch_shapes=scratch,
        compiler_params=pltpu.CompilerParams(vmem_limit_bytes=limit * 2**20),
        cost_estimate=pl.CostEstimate(flops=flops, bytes_accessed=moved, transcendentals=0),
    )


def run_pack(*args):
    return call(
        pack_kernel,
        [
            ((CHIPS, IN_ROWS, NOPE), bf16),
            ((8, BLOCKS), jnp.int32),
            ((8, QUERIES), jnp.int32),
        ],
        [VMEM] + [ANY] * 5,
        [
            pltpu.VMEM((LATENT + ROPE, ROWS), bf16),
            pltpu.VMEM((LATENT, HEADS * NOPE), bf16),
            pltpu.VMEM((LATENT, HEADS * VDIM), bf16),
            pltpu.VMEM((ROWS, HEADS * WIDTH_Q), bf16),
            pltpu.VMEM((ROWS, HEADS * VDIM), bf16),
            pltpu.VMEM((CHIPS, IN_ROWS, NOPE), bf16),
            pltpu.SemaphoreType.DMA((5,)),
            pltpu.SemaphoreType.DMA((SIDE,)),
        ],
        limit=60,
        out_specs=[ANY, VMEM, VMEM],
    )(*args)


def run_stats(*args):
    return call(
        stats_kernel,
        [
            ((KEYS, 2 * NOPE), bf16),
            ((KEYS, VDIM), bf16),
            ((QUERIES, 2 * NOPE), bf16),
            ((QUERIES, VDIM), bf16),
            ((8, QUERIES), f32),
        ],
        [SMEM] * 2 + [VMEM] * 3,
        [pltpu.VMEM((KEYS, NOPE), jnp.int32)],
    )(*args)


def run_gradient(*args):
    return call(
        gradient_kernel,
        [((CHIPS, OUT_ROWS, NOPE), bf16), ((CHIPS, KEY_ROWS, NOPE), bf16)],
        [SMEM] * 2 + [VMEM] * 7,
        [
            pltpu.VMEM((KEYS, NOPE), jnp.int32),
            pltpu.VMEM((KEYS, 2 * NOPE), bf16),
            pltpu.VMEM((KEYS, VDIM), bf16),
            pltpu.VMEM((QUERIES, 2 * NOPE), f32),
            pltpu.VMEM((CHUNK, 2 * NOPE), f32),
            pltpu.VMEM((CHUNK, VDIM), f32),
        ],
    )(*args)


def over_chips(slots):
    return lax.all_to_all(slots, ("y", "x"), 0, 0)


def swap(array, axis, bit):
    return lax.ppermute(array, axis, [(i, i ^ bit) for i in range(lax.axis_size(axis))])


def local(query, kv_row, w_uk, w_uv, grad_out, block_start):
    z_size = lax.axis_size("head")
    z_rows = ROWS // z_size
    kv_t = kv_row.T
    slots, meta, q_pos = run_pack(
        block_start.reshape(1, BLOCKS), kv_t, w_uk, w_uv, query, grad_out
    )
    own = over_chips(slots)
    other = swap(own[:, :KEY_ROWS], "core", 1)

    *placed, stats = run_stats(block_start, meta, q_pos, own, other)
    own_part, other_part = run_gradient(
        block_start, meta, q_pos, *placed, stats, swap(stats, "y", 1)
    )
    slots = over_chips(own_part.at[:, :KEY_ROWS].add(swap(other_part, "core", 1)))

    z_part = call(latent_kernel, [((ROWS, Z_WIDTH), bf16)], [VMEM] * 3)(slots, w_uk, w_uv)
    z_part, slots = lax.optimization_barrier((z_part, slots))
    grad_query, own_terms, other_terms = call(
        projection_kernel,
        [((ROWS, HEADS * WIDTH_Q), bf16)] + [((SIDE, SIDE, W_ROWS, W_WIDTH), bf16)] * 2,
        [VMEM] * 2,
        [pltpu.VMEM((LATENT, W_WIDTH), bf16)],
        flops=2 * ROWS * LATENT * W_WIDTH,
        moved=8 * 2**20,
    )(slots, kv_t)
    terms = own_terms + swap(other_terms, "core", 1)
    for axis in ("x", "y"):
        total = terms[0].astype(f32)
        for bit in range(1, SIDE):
            total = total + swap(terms[bit], axis, bit).astype(f32)
        terms = total.astype(bf16)

    z_slots = lax.all_to_all(z_part.reshape(z_size, z_rows, Z_WIDTH), "head", 0, 0)
    first_row = lax.axis_index("head") * z_rows
    kv_rows = lax.dynamic_slice_in_dim(kv_row, first_row, z_rows)
    rows = call(norm_kernel, [((z_size, z_rows, Z_WIDTH), bf16)], [VMEM] * 2)(z_slots, kv_rows)
    all_rows = lax.all_to_all(rows, "head", 0, 0).reshape(ROWS, Z_WIDTH)
    grad_kv_row = all_rows[:, : LATENT + ROPE].astype(f32)
    width = HEADS * NOPE
    return (grad_query, grad_kv_row, total[:, :width], total[:, width:])


def solution(mesh):
    axes = ("y", "x", "core")
    devices = mesh.devices.reshape(SIDE, SIDE, 2, mesh.shape["head"])
    placed = (
        P(axes, "head"),
        P(axes, None),
        P(None, "head"),
        P(None, "head"),
        P(axes, "head"),
        P(),
    )
    return jax.shard_map(
        local,
        mesh=Mesh(devices, (*axes, "head")),
        in_specs=placed,
        out_specs=(P(axes, "head"), P(axes, None), P(axes, "head"), P(axes, "head")),
        check_vma=False,
    )
```

```python
import math

import jax
import jax.numpy as jnp
from jax import lax
from jax.experimental import pallas as pl
from jax.experimental.pallas import tpu as pltpu
from jax.sharding import Mesh
from jax.sharding import PartitionSpec as P

LATENT = 512
ROPE = 64
NOPE = 128
VDIM = 128
WIDTH_Q = NOPE + ROPE
HALF = 64
BLOCKS = 64
HEADS = 4
SIDE = 4
CHIPS = SIDE * SIDE
PIECE = HALF // 2
ROWS = 2 * HALF
KEYS = 2 * CHIPS * HALF
QUERIES = 2 * CHIPS * PIECE
KEY_ROWS = 2 * HALF + PIECE
IN_ROWS = KEY_ROWS + 5 * PIECE
OUT_ROWS = KEY_ROWS + 3 * PIECE
W_ROWS = LATENT // (2 * CHIPS)
W_WIDTH = HEADS * (NOPE + VDIM)
CHUNK = 1024
GROUP = 512
N_CHUNKS = KEYS // CHUNK
N_GROUPS = QUERIES // GROUP
UNROLL = CHIPS
Z_WIDTH = 640
LOG2E = 1.4426950408889634
SCALE = 1.0 / math.sqrt(WIDTH_Q)

eps = 1e-06
masked_low = -1e30
bf16 = jnp.bfloat16
f32 = jnp.float32
VMEM = pl.BlockSpec(memory_space=pltpu.VMEM)
SMEM = pl.BlockSpec(memory_space=pltpu.SMEM)
ANY = pl.BlockSpec(memory_space=pl.ANY)


def dot(left, right, left_dim=1, right_dim=0):
    return lax.dot_general(
        left, right, (((left_dim,), (right_dim,)), ((), ())), preferred_element_type=f32
    )


def rms_rows(latent):
    values = latent.astype(f32)
    inverse = lax.rsqrt(jnp.mean(values * values, axis=-1, keepdims=True) + eps)
    return (values * inverse, inverse)


def list_blocks(starts, meta, q_pos):
    half = lax.axis_index("y") % 2
    core = lax.axis_index("core")
    shape = (BLOCKS, BLOCKS)
    across = jnp.broadcast_to(starts[...], shape)
    down = across.T
    row = lax.broadcasted_iota(jnp.int32, shape, 0)
    lane = lax.broadcasted_iota(jnp.int32, shape, 1)

    def tally(where, axis):
        return jnp.sum(where.astype(jnp.int32), axis=axis, keepdims=True)

    key_rank = tally((down < across) & (row % 2 == half), 0)
    query_rank = tally((down < across) & ((row // 2) % 2 == core), 0)
    query_rank_down = tally((across < down) & ((lane // 2) % 2 == core), 1)
    is_query = (row[:, :1] // 2) % 2 == core
    shape = (BLOCKS, QUERIES)
    piece = lax.broadcasted_iota(jnp.int32, shape, 1) // PIECE
    mine = (query_rank_down == piece) & is_query
    position = jnp.sum(jnp.where(mine, down[:, :1], 0), axis=0, keepdims=True)
    seen = []
    for group in range(N_GROUPS):
        last = position[:, (group + 1) * GROUP - 1 : (group + 1) * GROUP]
        seen.append(tally((across[:1] <= last) & (lane[:1] % 2 == half), 1))
    seen = jnp.concatenate(seen + [jnp.zeros((1, BLOCKS - N_GROUPS), jnp.int32)], axis=1)
    rest = jnp.zeros((5, BLOCKS), jnp.int32)
    meta[...] = jnp.concatenate([key_rank, query_rank, seen, rest], axis=0)
    offset = lax.broadcasted_iota(jnp.int32, (1, QUERIES), 1) % PIECE
    offset = offset + (lax.axis_index("y") // 2) * PIECE
    q_pos[...] = jnp.broadcast_to(position + offset, q_pos.shape)


def pack_kernel(
    block_start,
    kv_any,
    wk_any,
    wv_any,
    q_any,
    g_any,
    out_any,
    meta,
    q_pos,
    kv_ref,
    wk_ref,
    wv_ref,
    q_ref,
    g_ref,
    out_ref,
    sems,
    out_sems,
):
    pairs = [(q_any, q_ref), (g_any, g_ref), (kv_any, kv_ref), (wk_any, wk_ref), (wv_any, wv_ref)]
    copies = [
        pltpu.make_async_copy(source, target, sems.at[index])
        for index, (source, target) in enumerate(pairs)
    ]
    for copy in copies:
        copy.start()
    list_blocks(block_start, meta, q_pos)
    copies[0].wait()
    copies[1].wait()
    for x in range(HEADS):
        q_nope = q_ref[:, x * WIDTH_Q : x * WIDTH_Q + NOPE]
        q_rope = q_ref[:, x * WIDTH_Q + NOPE : (x + 1) * WIDTH_Q]
        grad = g_ref[:, x * VDIM : (x + 1) * VDIM]
        for y in range(SIDE):
            slot = y * SIDE + x
            first = slice((y // 2) * PIECE, (y // 2 + 1) * PIECE)
            second = slice(HALF + (y // 2) * PIECE, HALF + (y // 2 + 1) * PIECE)
            low = KEY_ROWS
            out_ref[slot, low : low + PIECE] = q_nope[first]
            out_ref[slot, low + PIECE : low + 2 * PIECE] = q_nope[second]
            out_ref[slot, low + 2 * PIECE : low + 3 * PIECE] = grad[first]
            out_ref[slot, low + 3 * PIECE : low + 4 * PIECE] = grad[second]
            out_ref[slot, low + 4 * PIECE : low + 5 * PIECE] = jnp.concatenate(
                [q_rope[first], q_rope[second]], axis=1
            )
    copies[2].wait()
    values = kv_ref[:LATENT, :].astype(f32)
    inverse = lax.rsqrt(jnp.mean(values * values, axis=0, keepdims=True) + eps)
    normed = (values * inverse).T.astype(bf16)
    rope = kv_ref[LATENT:, :].astype(f32).T.astype(bf16)
    copies[3].wait()
    keys = dot(normed, wk_ref[...]).astype(bf16)
    copies[4].wait()
    values = dot(normed, wv_ref[...]).astype(bf16)
    sent = []
    for y in range(SIDE):
        low = (y % 2) * HALF
        for x in range(HEADS):
            slot = y * SIDE + x
            out_ref[slot, :HALF] = keys[low : low + HALF, x * NOPE : (x + 1) * NOPE]
            out_ref[slot, HALF : 2 * HALF] = values[low : low + HALF, x * VDIM : (x + 1) * VDIM]
            out_ref[slot, 2 * HALF : KEY_ROWS] = jnp.concatenate(
                [rope[low : low + PIECE], rope[low + PIECE : low + HALF]], axis=1
            )
        part = pl.ds(y * SIDE, SIDE)
        sent.append(pltpu.make_async_copy(out_ref.at[part], out_any.at[part], out_sems.at[y]))
        sent[-1].start()
    for copy in sent:
        copy.wait()


def key_block(chip, core):
    return (2 * chip + core) * 2 + lax.axis_index("y") % 2


def place_positions(block_start, meta, k_pos):
    rows = lax.broadcasted_iota(jnp.int32, (HALF, NOPE), 0)

    def body(index, carry):
        block = 2 * index + lax.axis_index("y") % 2
        at = pl.ds(pl.multiple_of(meta[0, block] * HALF, HALF), HALF)
        k_pos[at, :] = rows + block_start[block]
        return carry

    lax.fori_loop(0, 2 * CHIPS, body, 0, unroll=UNROLL)


def seen_chunks(meta, group):
    return (meta[2, group] * HALF + CHUNK - 1) // CHUNK


def place_kernel(block_start, meta, own_ref, queries, grads, k_pos):
    core = lax.axis_index("core")
    pad = jnp.zeros((PIECE, HALF), bf16)

    def place(chip, carry):
        low = KEY_ROWS
        q_rope = own_ref[chip, low + 4 * PIECE : low + 5 * PIECE]
        for half in range(2):
            rank = meta[1, (2 * chip + core) * 2 + half]
            at = pl.ds(pl.multiple_of(rank * PIECE, PIECE), PIECE)
            queries[at, :NOPE] = own_ref[chip, low + half * PIECE : low + (half + 1) * PIECE]
            queries[at, NOPE:] = jnp.concatenate(
                [q_rope[:, half * HALF : (half + 1) * HALF], pad], axis=1
            )
            grads[at, :] = own_ref[chip, low + (2 + half) * PIECE : low + (3 + half) * PIECE]
        return carry

    lax.fori_loop(0, CHIPS, place, 0, unroll=UNROLL)
    place_positions(block_start, meta, k_pos)


def stats_kernel(
    meta,
    q_pos,
    own_ref,
    other_ref,
    queries,
    grads,
    k_pos,
    keys,
    stats,
    scores,
    slopes,
    values,
):
    core = lax.axis_index("core")
    pad = jnp.zeros((HALF, HALF), bf16)

    def place(chip, carry):
        for ref, side in ((own_ref, core), (other_ref, 1 - core)):
            rank = meta[0, key_block(chip, side)]
            at = pl.ds(pl.multiple_of(rank * HALF, HALF), HALF)
            rope = ref[chip, 2 * HALF : KEY_ROWS]
            rope = jnp.concatenate([rope[:, :HALF], rope[:, HALF:]], axis=0)
            keys[at, :NOPE] = ref[chip, :HALF]
            keys[at, NOPE:] = jnp.concatenate([rope, pad], axis=1)
            values[at, :] = ref[chip, HALF : 2 * HALF]
        return carry

    lax.fori_loop(0, CHIPS, place, 0, unroll=UNROLL)

    for group in range(N_GROUPS):
        lanes = slice(group * GROUP, (group + 1) * GROUP)
        q_group = queries[lanes, :]
        g_group = grads[lanes, :]
        q_at = q_pos[0:1, lanes]

        def gather_stats(index, carry):
            top, weight_sum, weighted = carry
            at = pl.ds(pl.multiple_of(index * CHUNK, CHUNK), CHUNK)
            score = dot(keys[at, :], q_group, 1, 1) * (SCALE * LOG2E)
            key_at = jnp.concatenate([k_pos[at, :]] * (GROUP // NOPE), axis=1)
            score = jnp.where(key_at <= q_at, score, masked_low)
            slope = dot(values[at, :], g_group, 1, 1)
            scores[at, lanes] = score
            slopes[at, lanes] = slope
            fresh = jnp.maximum(top, jnp.max(score, axis=0, keepdims=True))
            fade = jnp.exp2(top - fresh)
            weight = jnp.exp2(score - fresh)
            weight_sum = weight_sum * fade + jnp.sum(weight, axis=0, keepdims=True)
            weighted = weighted * fade + jnp.sum(weight * slope, axis=0, keepdims=True)
            return (fresh, weight_sum, weighted)

        zero = jnp.zeros((1, GROUP), f32)
        top, weight_sum, weighted = lax.fori_loop(
            0,
            seen_chunks(meta, group),
            gather_stats,
            (jnp.full((1, GROUP), masked_low, f32), zero, zero),
        )
        stats[:, lanes] = jnp.concatenate(
            [top, weight_sum, weighted, jnp.zeros((5, GROUP), f32)], axis=0
        )


def gradient_kernel(
    meta,
    keys,
    queries,
    grads,
    scores,
    slopes,
    own_stats,
    other_stats,
    own_out,
    other_out,
    key_grads,
    value_grads,
    query_grads,
    key_sum,
    value_sum,
):
    own_top = own_stats[0:1, :]
    other_top = other_stats[0:1, :]
    top = jnp.maximum(own_top, other_top)
    own_fade = jnp.exp2(own_top - top)
    other_fade = jnp.exp2(other_top - top)
    weight_sum = own_stats[1:2, :] * own_fade + other_stats[1:2, :] * other_fade
    weighted = own_stats[2:3, :] * own_fade + other_stats[2:3, :] * other_fade
    log_total = top + jnp.log2(weight_sum)
    average = weighted / weight_sum
    query_grads[...] = jnp.zeros_like(query_grads)

    def gradients(index, carry):
        at = pl.ds(pl.multiple_of(index * CHUNK, CHUNK), CHUNK)
        key_sum[...] = jnp.zeros_like(key_sum)
        value_sum[...] = jnp.zeros_like(value_sum)
        for group in range(N_GROUPS):
            lanes = slice(group * GROUP, (group + 1) * GROUP)

            @pl.when(index < seen_chunks(meta, group))
            def _(lanes=lanes):
                probs = jnp.exp2(scores[at, lanes] - log_total[:, lanes])
                slope = (slopes[at, lanes] - average[:, lanes]) * SCALE
                score_grad = (probs * slope).astype(bf16)
                value_sum[...] += dot(probs.astype(bf16), grads[lanes, :])
                key_sum[...] += dot(score_grad, queries[lanes, :])
                query_grads[lanes, :] += dot(score_grad, keys[at, :], 0, 0)

        key_grads[at, :] = key_sum[...].astype(bf16)
        value_grads[at, :] = value_sum[...].astype(bf16)
        return carry

    lax.fori_loop(0, N_CHUNKS, gradients, 0)
    core = lax.axis_index("core")

    def hand_out(chip, carry):
        for ref, side in ((own_out, core), (other_out, 1 - core)):
            rank = meta[0, key_block(chip, side)]
            at = pl.ds(pl.multiple_of(rank * HALF, HALF), HALF)
            ref[chip, :HALF] = key_grads[at, :NOPE]
            ref[chip, HALF : 2 * HALF] = value_grads[at, :]
            rope = key_grads[at, NOPE:WIDTH_Q]
            ref[chip, 2 * HALF : KEY_ROWS] = jnp.concatenate([rope[:PIECE], rope[PIECE:]], axis=1)
        low = KEY_ROWS
        ropes = []
        for half in range(2):
            rank = meta[1, (2 * chip + core) * 2 + half]
            at = pl.ds(pl.multiple_of(rank * PIECE, PIECE), PIECE)
            piece = query_grads[at, :].astype(bf16)
            own_out[chip, low + half * PIECE : low + (half + 1) * PIECE] = piece[:, :NOPE]
            ropes.append(piece[:, NOPE:WIDTH_Q])
        own_out[chip, low + 2 * PIECE : low + 3 * PIECE] = jnp.concatenate(ropes, axis=1)
        return carry

    lax.fori_loop(0, CHIPS, hand_out, 0, unroll=UNROLL)


def slot_sum(slots_ref, slots, low, rows):
    total = slots_ref[slots[0], low : low + rows].astype(f32)
    for slot in slots[1:]:
        total = total + slots_ref[slot, low : low + rows].astype(f32)
    return total


def head_sums(slots_ref, low):
    parts = []
    for x in range(HEADS):
        halves = [
            slot_sum(slots_ref, (y * SIDE + x, (y + 2) * SIDE + x), low, HALF) for y in range(2)
        ]
        parts.append(jnp.concatenate(halves, axis=0).astype(bf16))
    return jnp.concatenate(parts, axis=1)


def latent_kernel(
    slots_ref, wk_ref, wv_ref, kv_ref, out_ref, grad_q_ref, own_ref, other_ref, terms
):
    key_flat = head_sums(slots_ref, 0)
    value_flat = head_sums(slots_ref, HALF)
    latent = dot(key_flat, wk_ref[...], 1, 1) + dot(value_flat, wv_ref[...], 1, 1)
    out_ref[:, :LATENT] = latent.astype(bf16)
    ropes = []
    for y in range(2):
        slots = [row * SIDE + x for row in (y, y + 2) for x in range(HEADS)]
        rope = slot_sum(slots_ref, slots, 2 * HALF, PIECE)
        ropes += [rope[:, :HALF], rope[:, HALF:]]
    rope = jnp.concatenate(ropes, axis=0)
    out_ref[:, LATENT:] = jnp.concatenate([rope, jnp.zeros_like(rope)], axis=1).astype(bf16)
    values = kv_ref[:LATENT, :].astype(f32)
    inverse = lax.rsqrt(jnp.mean(values * values, axis=0, keepdims=True) + eps)
    normed = (values * inverse).astype(bf16)
    terms[:, : HEADS * NOPE] = dot(normed, key_flat).astype(bf16)
    terms[:, HEADS * NOPE :] = dot(normed, value_flat).astype(bf16)
    core = lax.axis_index("core")
    y_here, x_here = lax.axis_index("y"), lax.axis_index("x")
    for dx in range(SIDE):
        for dy in range(SIDE):
            chip = (y_here ^ dy) * SIDE + (x_here ^ dx)
            first = pl.multiple_of((2 * chip + core) * W_ROWS, W_ROWS)
            second = pl.multiple_of((2 * chip + 1 - core) * W_ROWS, W_ROWS)
            own_ref[dx, dy] = terms[pl.ds(first, W_ROWS), :]
            other_ref[dx, dy] = terms[pl.ds(second, W_ROWS), :]
    low = KEY_ROWS
    for quarter in range(2):
        for half in range(2):
            parts = []
            for x in range(HEADS):
                slots = (2 * quarter * SIDE + x, (2 * quarter + 1) * SIDE + x)
                parts.append(slot_sum(slots_ref, slots, low + half * PIECE, PIECE))
                rope = slot_sum(slots_ref, slots, low + 2 * PIECE, PIECE)
                parts.append(rope[:, half * HALF : (half + 1) * HALF])
            first = half * HALF + quarter * PIECE
            grad_q_ref[first : first + PIECE, :] = jnp.concatenate(parts, axis=1).astype(bf16)


def norm_kernel(slots_ref, kv_ref, out_ref):
    total = jnp.sum(slots_ref[...].astype(f32), axis=0)
    x_hat, inverse = rms_rows(kv_ref[:, :LATENT])
    latent = total[:, :LATENT]
    latent = inverse * (latent - x_hat * jnp.mean(latent * x_hat, axis=-1, keepdims=True))
    row = jnp.concatenate([latent, total[:, LATENT:]], axis=1).astype(bf16)
    out_ref[...] = jnp.broadcast_to(row[None], out_ref.shape)


def call(kernel, shapes, specs, scratch=(), limit=32, flops=0, moved=0, out_specs=None):
    shapes = [jax.ShapeDtypeStruct(*shape) for shape in shapes]
    single = len(shapes) == 1
    if out_specs is None:
        out_specs = VMEM if single else [VMEM] * len(shapes)
    return pl.pallas_call(
        kernel,
        out_shape=shapes[0] if single else shapes,
        in_specs=specs,
        out_specs=out_specs,
        scratch_shapes=scratch,
        compiler_params=pltpu.CompilerParams(vmem_limit_bytes=limit * 2**20),
        cost_estimate=pl.CostEstimate(flops=flops, bytes_accessed=moved, transcendentals=0),
    )


def run_pack(*args):
    return call(
        pack_kernel,
        [
            ((CHIPS, IN_ROWS, NOPE), bf16),
            ((8, BLOCKS), jnp.int32),
            ((8, QUERIES), jnp.int32),
        ],
        [VMEM] + [ANY] * 5,
        [
            pltpu.VMEM((LATENT + ROPE, ROWS), bf16),
            pltpu.VMEM((LATENT, HEADS * NOPE), bf16),
            pltpu.VMEM((LATENT, HEADS * VDIM), bf16),
            pltpu.VMEM((ROWS, HEADS * WIDTH_Q), bf16),
            pltpu.VMEM((ROWS, HEADS * VDIM), bf16),
            pltpu.VMEM((CHIPS, IN_ROWS, NOPE), bf16),
            pltpu.SemaphoreType.DMA((5,)),
            pltpu.SemaphoreType.DMA((SIDE,)),
        ],
        limit=60,
        out_specs=[ANY, VMEM, VMEM],
    )(*args)


def run_place(*args):
    return call(
        place_kernel,
        [((QUERIES, 2 * NOPE), bf16), ((QUERIES, VDIM), bf16), ((KEYS, NOPE), jnp.int32)],
        [SMEM] * 2 + [VMEM],
        limit=16,
        flops=10**8,
        moved=4 * 2**20,
    )(*args)


def run_stats(*args):
    return call(
        stats_kernel,
        [
            ((KEYS, 2 * NOPE), bf16),
            ((8, QUERIES), f32),
            ((KEYS, QUERIES), f32),
            ((KEYS, QUERIES), f32),
        ],
        [SMEM] + [VMEM] * 6,
        [pltpu.VMEM((KEYS, VDIM), bf16)],
        limit=28,
    )(*args)


def run_gradient(*args):
    return call(
        gradient_kernel,
        [((CHIPS, OUT_ROWS, NOPE), bf16), ((CHIPS, KEY_ROWS, NOPE), bf16)],
        [SMEM] + [VMEM] * 7,
        [
            pltpu.VMEM((KEYS, 2 * NOPE), bf16),
            pltpu.VMEM((KEYS, VDIM), bf16),
            pltpu.VMEM((QUERIES, 2 * NOPE), f32),
            pltpu.VMEM((CHUNK, 2 * NOPE), f32),
            pltpu.VMEM((CHUNK, VDIM), f32),
        ],
        limit=28,
    )(*args)


def over_chips(slots):
    return lax.all_to_all(slots, ("y", "x"), 0, 0)


def swap(array, axis, bit):
    return lax.ppermute(array, axis, [(i, i ^ bit) for i in range(lax.axis_size(axis))])


def local(query, kv_row, w_uk, w_uv, grad_out, block_start):
    z_size = lax.axis_size("head")
    z_rows = ROWS // z_size
    kv_t = kv_row.T
    slots, meta, q_pos = run_pack(
        block_start.reshape(1, BLOCKS), kv_t, w_uk, w_uv, query, grad_out
    )
    own = over_chips(slots)
    other = swap(own[:, :KEY_ROWS], "core", 1)

    queries, grads, k_pos = run_place(block_start, meta, own)
    keys, stats, scores, slopes = run_stats(meta, q_pos, own, other, queries, grads, k_pos)
    own_part, other_part = run_gradient(
        meta, keys, queries, grads, scores, slopes, stats, swap(stats, "y", 1)
    )
    slots = over_chips(own_part.at[:, :KEY_ROWS].add(swap(other_part, "core", 1)))

    z_part, grad_query, own_terms, other_terms = call(
        latent_kernel,
        [((ROWS, Z_WIDTH), bf16), ((ROWS, HEADS * WIDTH_Q), bf16)]
        + [((SIDE, SIDE, W_ROWS, W_WIDTH), bf16)] * 2,
        [VMEM] * 4,
        [pltpu.VMEM((LATENT, W_WIDTH), bf16)],
    )(slots, w_uk, w_uv, kv_t)
    terms = own_terms + swap(other_terms, "core", 1)
    for axis in ("x", "y"):
        total = terms[0].astype(f32)
        for bit in range(1, SIDE):
            total = total + swap(terms[bit], axis, bit).astype(f32)
        terms = total.astype(bf16)

    z_slots = lax.all_to_all(z_part.reshape(z_size, z_rows, Z_WIDTH), "head", 0, 0)
    first_row = lax.axis_index("head") * z_rows
    kv_rows = lax.dynamic_slice_in_dim(kv_row, first_row, z_rows)
    rows = call(norm_kernel, [((z_size, z_rows, Z_WIDTH), bf16)], [VMEM] * 2)(z_slots, kv_rows)
    all_rows = lax.all_to_all(rows, "head", 0, 0).reshape(ROWS, Z_WIDTH)
    grad_kv_row = all_rows[:, : LATENT + ROPE].astype(f32)
    width = HEADS * NOPE
    return (grad_query, grad_kv_row, total[:, :width], total[:, width:])


def solution(mesh):
    axes = ("y", "x", "core")
    devices = mesh.devices.reshape(SIDE, SIDE, 2, mesh.shape["head"])
    placed = (
        P(axes, "head"),
        P(axes, None),
        P(None, "head"),
        P(None, "head"),
        P(axes, "head"),
        P(),
    )
    return jax.shard_map(
        local,
        mesh=Mesh(devices, (*axes, "head")),
        in_specs=placed,
        out_specs=(P(axes, "head"), P(axes, None), P(axes, "head"), P(axes, "head")),
        check_vma=False,
    )
```

```python
import math

import jax
import jax.numpy as jnp
from jax import lax
from jax.experimental import pallas as pl
from jax.experimental.pallas import tpu as pltpu
from jax.sharding import Mesh
from jax.sharding import PartitionSpec as P

LATENT = 512
ROPE = 64
NOPE = 128
VDIM = 128
WIDTH_Q = NOPE + ROPE
HALF = 64
BLOCKS = 64
HEADS = 4
SIDE = 4
CHIPS = SIDE * SIDE
PIECE = HALF // 2
ROWS = 2 * HALF
KEYS = 2 * CHIPS * HALF
QUERIES = 2 * CHIPS * PIECE
KEY_ROWS = 2 * HALF + PIECE
IN_ROWS = KEY_ROWS + 5 * PIECE
OUT_ROWS = KEY_ROWS + 3 * PIECE
W_ROWS = LATENT // (2 * CHIPS)
W_WIDTH = HEADS * (NOPE + VDIM)
CHUNK = 1024
GROUP = 512
N_CHUNKS = KEYS // CHUNK
N_GROUPS = QUERIES // GROUP
UNROLL = CHIPS
Z_WIDTH = 640
LOG2E = 1.4426950408889634
SCALE = 1.0 / math.sqrt(WIDTH_Q)

eps = 1e-06
masked_low = -1e30
bf16 = jnp.bfloat16
f32 = jnp.float32
VMEM = pl.BlockSpec(memory_space=pltpu.VMEM)
SMEM = pl.BlockSpec(memory_space=pltpu.SMEM)
ANY = pl.BlockSpec(memory_space=pl.ANY)


def dot(left, right, left_dim=1, right_dim=0):
    return lax.dot_general(
        left, right, (((left_dim,), (right_dim,)), ((), ())), preferred_element_type=f32
    )


def rms_rows(latent):
    values = latent.astype(f32)
    inverse = lax.rsqrt(jnp.mean(values * values, axis=-1, keepdims=True) + eps)
    return (values * inverse, inverse)


def list_blocks(starts, meta, q_pos):
    half = lax.axis_index("y") % 2
    core = lax.axis_index("core")
    shape = (BLOCKS, BLOCKS)
    across = jnp.broadcast_to(starts[...], shape)
    down = across.T
    row = lax.broadcasted_iota(jnp.int32, shape, 0)
    lane = lax.broadcasted_iota(jnp.int32, shape, 1)

    def tally(where, axis):
        return jnp.sum(where.astype(jnp.int32), axis=axis, keepdims=True)

    key_rank = tally((down < across) & (row % 2 == half), 0)
    query_rank = tally((down < across) & ((row // 2) % 2 == core), 0)
    query_rank_down = tally((across < down) & ((lane // 2) % 2 == core), 1)
    is_query = (row[:, :1] // 2) % 2 == core
    shape = (BLOCKS, QUERIES)
    piece = lax.broadcasted_iota(jnp.int32, shape, 1) // PIECE
    mine = (query_rank_down == piece) & is_query
    position = jnp.sum(jnp.where(mine, down[:, :1], 0), axis=0, keepdims=True)
    seen = []
    for group in range(N_GROUPS):
        last = position[:, (group + 1) * GROUP - 1 : (group + 1) * GROUP]
        seen.append(tally((across[:1] <= last) & (lane[:1] % 2 == half), 1))
    seen = jnp.concatenate(seen + [jnp.zeros((1, BLOCKS - N_GROUPS), jnp.int32)], axis=1)
    rest = jnp.zeros((5, BLOCKS), jnp.int32)
    meta[...] = jnp.concatenate([key_rank, query_rank, seen, rest], axis=0)
    offset = lax.broadcasted_iota(jnp.int32, (1, QUERIES), 1) % PIECE
    offset = offset + (lax.axis_index("y") // 2) * PIECE
    q_pos[...] = jnp.broadcast_to(position + offset, q_pos.shape)


def pack_kernel(
    block_start,
    kv_any,
    wk_any,
    wv_any,
    q_any,
    g_any,
    out_any,
    meta,
    q_pos,
    kv_ref,
    wk_ref,
    wv_ref,
    q_ref,
    g_ref,
    out_ref,
    sems,
    out_sems,
):
    pairs = [(q_any, q_ref), (g_any, g_ref), (kv_any, kv_ref), (wk_any, wk_ref), (wv_any, wv_ref)]
    copies = [
        pltpu.make_async_copy(source, target, sems.at[index])
        for index, (source, target) in enumerate(pairs)
    ]
    for copy in copies:
        copy.start()
    list_blocks(block_start, meta, q_pos)
    copies[0].wait()
    copies[1].wait()
    for x in range(HEADS):
        q_nope = q_ref[:, x * WIDTH_Q : x * WIDTH_Q + NOPE]
        q_rope = q_ref[:, x * WIDTH_Q + NOPE : (x + 1) * WIDTH_Q]
        grad = g_ref[:, x * VDIM : (x + 1) * VDIM]
        for y in range(SIDE):
            slot = y * SIDE + x
            first = slice((y // 2) * PIECE, (y // 2 + 1) * PIECE)
            second = slice(HALF + (y // 2) * PIECE, HALF + (y // 2 + 1) * PIECE)
            low = KEY_ROWS
            out_ref[slot, low : low + PIECE] = q_nope[first]
            out_ref[slot, low + PIECE : low + 2 * PIECE] = q_nope[second]
            out_ref[slot, low + 2 * PIECE : low + 3 * PIECE] = grad[first]
            out_ref[slot, low + 3 * PIECE : low + 4 * PIECE] = grad[second]
            out_ref[slot, low + 4 * PIECE : low + 5 * PIECE] = jnp.concatenate(
                [q_rope[first], q_rope[second]], axis=1
            )
    part = (slice(None), pl.ds(KEY_ROWS, IN_ROWS - KEY_ROWS))
    sent = [pltpu.make_async_copy(out_ref.at[part], out_any.at[part], out_sems.at[SIDE])]
    sent[0].start()
    copies[2].wait()
    values = kv_ref[:LATENT, :].astype(f32)
    inverse = lax.rsqrt(jnp.mean(values * values, axis=0, keepdims=True) + eps)
    normed = (values * inverse).T.astype(bf16)
    rope = kv_ref[LATENT:, :].astype(f32).T.astype(bf16)
    copies[3].wait()
    keys = dot(normed, wk_ref[...]).astype(bf16)
    copies[4].wait()
    values = dot(normed, wv_ref[...]).astype(bf16)
    for y in range(SIDE):
        low = (y % 2) * HALF
        for x in range(HEADS):
            slot = y * SIDE + x
            out_ref[slot, :HALF] = keys[low : low + HALF, x * NOPE : (x + 1) * NOPE]
            out_ref[slot, HALF : 2 * HALF] = values[low : low + HALF, x * VDIM : (x + 1) * VDIM]
            out_ref[slot, 2 * HALF : KEY_ROWS] = jnp.concatenate(
                [rope[low : low + PIECE], rope[low + PIECE : low + HALF]], axis=1
            )
        part = (pl.ds(y * SIDE, SIDE), pl.ds(0, KEY_ROWS))
        sent.append(pltpu.make_async_copy(out_ref.at[part], out_any.at[part], out_sems.at[y]))
        sent[-1].start()
    for copy in sent:
        copy.wait()


def key_block(chip, core):
    return (2 * chip + core) * 2 + lax.axis_index("y") % 2


def place_positions(block_start, meta, k_pos):
    rows = lax.broadcasted_iota(jnp.int32, (HALF, NOPE), 0)

    def body(index, carry):
        block = 2 * index + lax.axis_index("y") % 2
        at = pl.ds(pl.multiple_of(meta[0, block] * HALF, HALF), HALF)
        k_pos[at, :] = rows + block_start[block]
        return carry

    lax.fori_loop(0, 2 * CHIPS, body, 0, unroll=UNROLL)


def step_rows(group):
    return CHUNK // 2 if group == 0 else CHUNK


def seen_steps(meta, group):
    return (meta[2, group] * HALF + step_rows(group) - 1) // step_rows(group)


def place_kernel(block_start, meta, own_ref, queries, grads, k_pos):
    core = lax.axis_index("core")
    pad = jnp.zeros((PIECE, HALF), bf16)

    def place(chip, carry):
        low = KEY_ROWS
        q_rope = own_ref[chip, low + 4 * PIECE : low + 5 * PIECE]
        for half in range(2):
            rank = meta[1, (2 * chip + core) * 2 + half]
            at = pl.ds(pl.multiple_of(rank * PIECE, PIECE), PIECE)
            queries[at, :NOPE] = own_ref[chip, low + half * PIECE : low + (half + 1) * PIECE]
            queries[at, NOPE:] = jnp.concatenate(
                [q_rope[:, half * HALF : (half + 1) * HALF], pad], axis=1
            )
            grads[at, :] = own_ref[chip, low + (2 + half) * PIECE : low + (3 + half) * PIECE]
        return carry

    lax.fori_loop(0, CHIPS, place, 0, unroll=UNROLL)
    place_positions(block_start, meta, k_pos)


def stats_kernel(
    meta,
    q_pos,
    own_ref,
    other_ref,
    queries,
    grads,
    k_pos,
    keys,
    stats,
    scores,
    slopes,
    values,
):
    core = lax.axis_index("core")
    pad = jnp.zeros((HALF, HALF), bf16)

    def place(chip, carry):
        for ref, side in ((own_ref, core), (other_ref, 1 - core)):
            rank = meta[0, key_block(chip, side)]
            at = pl.ds(pl.multiple_of(rank * HALF, HALF), HALF)
            rope = ref[chip, 2 * HALF : KEY_ROWS]
            rope = jnp.concatenate([rope[:, :HALF], rope[:, HALF:]], axis=0)
            keys[at, :NOPE] = ref[chip, :HALF]
            keys[at, NOPE:] = jnp.concatenate([rope, pad], axis=1)
            values[at, :] = ref[chip, HALF : 2 * HALF]
        return carry

    lax.fori_loop(0, CHIPS, place, 0, unroll=UNROLL)

    for group in range(N_GROUPS):
        lanes = slice(group * GROUP, (group + 1) * GROUP)
        q_group = queries[lanes, :]
        g_group = grads[lanes, :]
        q_at = q_pos[0:1, lanes]

        rows = step_rows(group)

        def gather_stats(index, carry, lanes=lanes, rows=rows):
            top, weight_sum, weighted = carry
            at = pl.ds(pl.multiple_of(index * rows, rows), rows)
            score = dot(keys[at, :], q_group, 1, 1) * (SCALE * LOG2E)
            key_at = jnp.concatenate([k_pos[at, :]] * (GROUP // NOPE), axis=1)
            score = jnp.where(key_at <= q_at, score, masked_low)
            slope = dot(values[at, :], g_group, 1, 1)
            scores[at, lanes] = score
            slopes[at, lanes] = slope
            fresh = jnp.maximum(top, jnp.max(score, axis=0, keepdims=True))
            fade = jnp.exp2(top - fresh)
            weight = jnp.exp2(score - fresh)
            weight_sum = weight_sum * fade + jnp.sum(weight, axis=0, keepdims=True)
            weighted = weighted * fade + jnp.sum(weight * slope, axis=0, keepdims=True)
            return (fresh, weight_sum, weighted)

        zero = jnp.zeros((1, GROUP), f32)
        top, weight_sum, weighted = lax.fori_loop(
            0,
            seen_steps(meta, group),
            gather_stats,
            (jnp.full((1, GROUP), masked_low, f32), zero, zero),
        )
        stats[:, lanes] = jnp.concatenate(
            [top, weight_sum, weighted, jnp.zeros((5, GROUP), f32)], axis=0
        )


def gradient_kernel(
    meta,
    keys,
    queries,
    grads,
    scores,
    slopes,
    own_stats,
    other_stats,
    own_out,
    other_out,
    key_grads,
    value_grads,
    query_grads,
    key_sum,
    value_sum,
):
    own_top = own_stats[0:1, :]
    other_top = other_stats[0:1, :]
    top = jnp.maximum(own_top, other_top)
    own_fade = jnp.exp2(own_top - top)
    other_fade = jnp.exp2(other_top - top)
    weight_sum = own_stats[1:2, :] * own_fade + other_stats[1:2, :] * other_fade
    weighted = own_stats[2:3, :] * own_fade + other_stats[2:3, :] * other_fade
    log_total = top + jnp.log2(weight_sum)
    average = weighted / weight_sum
    query_grads[...] = jnp.zeros_like(query_grads)

    def gradients(index, carry):
        at = pl.ds(pl.multiple_of(index * CHUNK, CHUNK), CHUNK)
        key_sum[...] = jnp.zeros_like(key_sum)
        value_sum[...] = jnp.zeros_like(value_sum)
        for group in range(N_GROUPS):
            lanes = slice(group * GROUP, (group + 1) * GROUP)
            rows = step_rows(group)
            for step in range(CHUNK // rows):

                @pl.when(index * (CHUNK // rows) + step < seen_steps(meta, group))
                def _(lanes=lanes, rows=rows, step=step):
                    part = slice(step * rows, (step + 1) * rows)
                    at = pl.ds(pl.multiple_of(index * CHUNK + step * rows, rows), rows)
                    probs = jnp.exp2(scores[at, lanes] - log_total[:, lanes])
                    slope = (slopes[at, lanes] - average[:, lanes]) * SCALE
                    score_grad = (probs * slope).astype(bf16)
                    value_sum[part, :] += dot(probs.astype(bf16), grads[lanes, :])
                    key_sum[part, :] += dot(score_grad, queries[lanes, :])
                    query_grads[lanes, :] += dot(score_grad, keys[at, :], 0, 0)

        key_grads[at, :] = key_sum[...].astype(bf16)
        value_grads[at, :] = value_sum[...].astype(bf16)
        return carry

    lax.fori_loop(0, N_CHUNKS, gradients, 0)
    core = lax.axis_index("core")

    def hand_out(chip, carry):
        for ref, side in ((own_out, core), (other_out, 1 - core)):
            rank = meta[0, key_block(chip, side)]
            at = pl.ds(pl.multiple_of(rank * HALF, HALF), HALF)
            ref[chip, :HALF] = key_grads[at, :NOPE]
            ref[chip, HALF : 2 * HALF] = value_grads[at, :]
            rope = key_grads[at, NOPE:WIDTH_Q]
            ref[chip, 2 * HALF : KEY_ROWS] = jnp.concatenate([rope[:PIECE], rope[PIECE:]], axis=1)
        low = KEY_ROWS
        ropes = []
        for half in range(2):
            rank = meta[1, (2 * chip + core) * 2 + half]
            at = pl.ds(pl.multiple_of(rank * PIECE, PIECE), PIECE)
            piece = query_grads[at, :].astype(bf16)
            own_out[chip, low + half * PIECE : low + (half + 1) * PIECE] = piece[:, :NOPE]
            ropes.append(piece[:, NOPE:WIDTH_Q])
        own_out[chip, low + 2 * PIECE : low + 3 * PIECE] = jnp.concatenate(ropes, axis=1)
        return carry

    lax.fori_loop(0, CHIPS, hand_out, 0, unroll=UNROLL)


def slot_sum(slots_ref, slots, low, rows):
    total = slots_ref[slots[0], low : low + rows].astype(f32)
    for slot in slots[1:]:
        total = total + slots_ref[slot, low : low + rows].astype(f32)
    return total


def head_sums(slots_ref, low):
    parts = []
    for x in range(HEADS):
        halves = [
            slot_sum(slots_ref, (y * SIDE + x, (y + 2) * SIDE + x), low, HALF) for y in range(2)
        ]
        parts.append(jnp.concatenate(halves, axis=0).astype(bf16))
    return jnp.concatenate(parts, axis=1)


def latent_kernel(
    slots_ref, wk_ref, wv_ref, kv_ref, out_ref, grad_q_ref, own_ref, other_ref, terms
):
    key_flat = head_sums(slots_ref, 0)
    value_flat = head_sums(slots_ref, HALF)
    latent = dot(key_flat, wk_ref[...], 1, 1) + dot(value_flat, wv_ref[...], 1, 1)
    out_ref[:, :LATENT] = latent.astype(bf16)
    ropes = []
    for y in range(2):
        slots = [row * SIDE + x for row in (y, y + 2) for x in range(HEADS)]
        rope = slot_sum(slots_ref, slots, 2 * HALF, PIECE)
        ropes += [rope[:, :HALF], rope[:, HALF:]]
    rope = jnp.concatenate(ropes, axis=0)
    out_ref[:, LATENT:] = jnp.concatenate([rope, jnp.zeros_like(rope)], axis=1).astype(bf16)
    values = kv_ref[:LATENT, :].astype(f32)
    inverse = lax.rsqrt(jnp.mean(values * values, axis=0, keepdims=True) + eps)
    normed = (values * inverse).astype(bf16)
    terms[:, : HEADS * NOPE] = dot(normed, key_flat).astype(bf16)
    terms[:, HEADS * NOPE :] = dot(normed, value_flat).astype(bf16)
    core = lax.axis_index("core")
    y_here, x_here = lax.axis_index("y"), lax.axis_index("x")
    for dx in range(SIDE):
        for dy in range(SIDE):
            chip = (y_here ^ dy) * SIDE + (x_here ^ dx)
            first = pl.multiple_of((2 * chip + core) * W_ROWS, W_ROWS)
            second = pl.multiple_of((2 * chip + 1 - core) * W_ROWS, W_ROWS)
            own_ref[dx, dy] = terms[pl.ds(first, W_ROWS), :]
            other_ref[dx, dy] = terms[pl.ds(second, W_ROWS), :]
    low = KEY_ROWS
    for quarter in range(2):
        for half in range(2):
            parts = []
            for x in range(HEADS):
                slots = (2 * quarter * SIDE + x, (2 * quarter + 1) * SIDE + x)
                parts.append(slot_sum(slots_ref, slots, low + half * PIECE, PIECE))
                rope = slot_sum(slots_ref, slots, low + 2 * PIECE, PIECE)
                parts.append(rope[:, half * HALF : (half + 1) * HALF])
            first = half * HALF + quarter * PIECE
            grad_q_ref[first : first + PIECE, :] = jnp.concatenate(parts, axis=1).astype(bf16)


def norm_kernel(slots_ref, kv_ref, out_ref):
    total = jnp.sum(slots_ref[...].astype(f32), axis=0)
    x_hat, inverse = rms_rows(kv_ref[:, :LATENT])
    latent = total[:, :LATENT]
    latent = inverse * (latent - x_hat * jnp.mean(latent * x_hat, axis=-1, keepdims=True))
    row = jnp.concatenate([latent, total[:, LATENT:]], axis=1).astype(bf16)
    out_ref[...] = jnp.broadcast_to(row[None], out_ref.shape)


def call(kernel, shapes, specs, scratch=(), limit=32, flops=0, moved=0, out_specs=None):
    shapes = [jax.ShapeDtypeStruct(*shape) for shape in shapes]
    single = len(shapes) == 1
    if out_specs is None:
        out_specs = VMEM if single else [VMEM] * len(shapes)
    return pl.pallas_call(
        kernel,
        out_shape=shapes[0] if single else shapes,
        in_specs=specs,
        out_specs=out_specs,
        scratch_shapes=scratch,
        compiler_params=pltpu.CompilerParams(vmem_limit_bytes=limit * 2**20),
        cost_estimate=pl.CostEstimate(flops=flops, bytes_accessed=moved, transcendentals=0),
    )


def run_pack(*args):
    return call(
        pack_kernel,
        [
            ((CHIPS, IN_ROWS, NOPE), bf16),
            ((8, BLOCKS), jnp.int32),
            ((8, QUERIES), jnp.int32),
        ],
        [VMEM] + [ANY] * 5,
        [
            pltpu.VMEM((LATENT + ROPE, ROWS), bf16),
            pltpu.VMEM((LATENT, HEADS * NOPE), bf16),
            pltpu.VMEM((LATENT, HEADS * VDIM), bf16),
            pltpu.VMEM((ROWS, HEADS * WIDTH_Q), bf16),
            pltpu.VMEM((ROWS, HEADS * VDIM), bf16),
            pltpu.VMEM((CHIPS, IN_ROWS, NOPE), bf16),
            pltpu.SemaphoreType.DMA((5,)),
            pltpu.SemaphoreType.DMA((SIDE + 1,)),
        ],
        limit=60,
        out_specs=[ANY, VMEM, VMEM],
    )(*args)


def run_place(*args):
    return call(
        place_kernel,
        [((QUERIES, 2 * NOPE), bf16), ((QUERIES, VDIM), bf16), ((KEYS, NOPE), jnp.int32)],
        [SMEM] * 2 + [VMEM],
        limit=16,
        flops=10**8,
        moved=4 * 2**20,
    )(*args)


def run_stats(*args):
    return call(
        stats_kernel,
        [
            ((KEYS, 2 * NOPE), bf16),
            ((8, QUERIES), f32),
            ((KEYS, QUERIES), f32),
            ((KEYS, QUERIES), f32),
        ],
        [SMEM] + [VMEM] * 6,
        [pltpu.VMEM((KEYS, VDIM), bf16)],
        limit=28,
    )(*args)


def run_gradient(*args):
    return call(
        gradient_kernel,
        [((CHIPS, OUT_ROWS, NOPE), bf16), ((CHIPS, KEY_ROWS, NOPE), bf16)],
        [SMEM] + [VMEM] * 7,
        [
            pltpu.VMEM((KEYS, 2 * NOPE), bf16),
            pltpu.VMEM((KEYS, VDIM), bf16),
            pltpu.VMEM((QUERIES, 2 * NOPE), f32),
            pltpu.VMEM((CHUNK, 2 * NOPE), f32),
            pltpu.VMEM((CHUNK, VDIM), f32),
        ],
        limit=28,
    )(*args)


def over_chips(slots):
    return lax.all_to_all(slots, ("y", "x"), 0, 0)


def swap(array, axis, bit):
    return lax.ppermute(array, axis, [(i, i ^ bit) for i in range(lax.axis_size(axis))])


def local(query, kv_row, w_uk, w_uv, grad_out, block_start):
    z_size = lax.axis_size("head")
    z_rows = ROWS // z_size
    kv_t = kv_row.T
    slots, meta, q_pos = run_pack(
        block_start.reshape(1, BLOCKS), kv_t, w_uk, w_uv, query, grad_out
    )
    own = over_chips(slots)
    other = swap(own[:, :KEY_ROWS], "core", 1)

    queries, grads, k_pos = run_place(block_start, meta, own)
    keys, stats, scores, slopes = run_stats(meta, q_pos, own, other, queries, grads, k_pos)
    own_part, other_part = run_gradient(
        meta, keys, queries, grads, scores, slopes, stats, swap(stats, "y", 1)
    )
    slots = over_chips(own_part.at[:, :KEY_ROWS].add(swap(other_part, "core", 1)))

    z_part, grad_query, own_terms, other_terms = call(
        latent_kernel,
        [((ROWS, Z_WIDTH), bf16), ((ROWS, HEADS * WIDTH_Q), bf16)]
        + [((SIDE, SIDE, W_ROWS, W_WIDTH), bf16)] * 2,
        [VMEM] * 4,
        [pltpu.VMEM((LATENT, W_WIDTH), bf16)],
    )(slots, w_uk, w_uv, kv_t)
    terms = own_terms + swap(other_terms, "core", 1)
    for axis in ("x", "y"):
        total = terms[0].astype(f32)
        for bit in range(1, SIDE):
            total = total + swap(terms[bit], axis, bit).astype(f32)
        terms = total.astype(bf16)

    z_slots = lax.all_to_all(z_part.reshape(z_size, z_rows, Z_WIDTH), "head", 0, 0)
    first_row = lax.axis_index("head") * z_rows
    kv_rows = lax.dynamic_slice_in_dim(kv_row, first_row, z_rows)
    rows = call(norm_kernel, [((z_size, z_rows, Z_WIDTH), bf16)], [VMEM] * 2)(z_slots, kv_rows)
    all_rows = lax.all_to_all(rows, "head", 0, 0).reshape(ROWS, Z_WIDTH)
    grad_kv_row = all_rows[:, : LATENT + ROPE].astype(f32)
    width = HEADS * NOPE
    return (grad_query, grad_kv_row, total[:, :width], total[:, width:])


def solution(mesh):
    axes = ("y", "x", "core")
    devices = mesh.devices.reshape(SIDE, SIDE, 2, mesh.shape["head"])
    placed = (
        P(axes, "head"),
        P(axes, None),
        P(None, "head"),
        P(None, "head"),
        P(axes, "head"),
        P(),
    )
    return jax.shard_map(
        local,
        mesh=Mesh(devices, (*axes, "head")),
        in_specs=placed,
        out_specs=(P(axes, "head"), P(axes, None), P(axes, "head"), P(axes, "head")),
        check_vma=False,
    )
```

```python
import math

import jax
import jax.numpy as jnp
from jax import lax
from jax.experimental import pallas as pl
from jax.experimental.pallas import tpu as pltpu
from jax.sharding import Mesh
from jax.sharding import PartitionSpec as P

LATENT = 512
ROPE = 64
NOPE = 128
VDIM = 128
WIDTH_Q = NOPE + ROPE
HALF = 64
BLOCKS = 64
HEADS = 4
SIDE = 4
CHIPS = SIDE * SIDE
PIECE = HALF // 2
ROWS = 2 * HALF
KEYS = 2 * CHIPS * HALF
QUERIES = 2 * CHIPS * PIECE
KEY_ROWS = 2 * HALF + PIECE
IN_ROWS = KEY_ROWS + 5 * PIECE
OUT_ROWS = KEY_ROWS + 3 * PIECE
W_ROWS = LATENT // (2 * CHIPS)
W_WIDTH = HEADS * (NOPE + VDIM)
CHUNK = 1024
GROUP = 512
N_CHUNKS = KEYS // CHUNK
N_GROUPS = QUERIES // GROUP
UNROLL = CHIPS
Z_WIDTH = 640
LOG2E = 1.4426950408889634
SCALE = 1.0 / math.sqrt(WIDTH_Q)

eps = 1e-06
masked_low = -1e30
bf16 = jnp.bfloat16
f32 = jnp.float32
VMEM = pl.BlockSpec(memory_space=pltpu.VMEM)
SMEM = pl.BlockSpec(memory_space=pltpu.SMEM)
ANY = pl.BlockSpec(memory_space=pl.ANY)


def dot(left, right, left_dim=1, right_dim=0):
    return lax.dot_general(
        left, right, (((left_dim,), (right_dim,)), ((), ())), preferred_element_type=f32
    )


def rms_rows(latent):
    values = latent.astype(f32)
    inverse = lax.rsqrt(jnp.mean(values * values, axis=-1, keepdims=True) + eps)
    return (values * inverse, inverse)


def list_blocks(starts, meta, q_pos):
    half = lax.axis_index("y") % 2
    core = lax.axis_index("core")
    shape = (BLOCKS, BLOCKS)
    across = jnp.broadcast_to(starts[...], shape)
    down = across.T
    row = lax.broadcasted_iota(jnp.int32, shape, 0)
    lane = lax.broadcasted_iota(jnp.int32, shape, 1)

    def tally(where, axis):
        return jnp.sum(where.astype(jnp.int32), axis=axis, keepdims=True)

    key_rank = tally((down < across) & (row % 2 == half), 0)
    query_rank = tally((down < across) & ((row // 2) % 2 == core), 0)
    query_rank_down = tally((across < down) & ((lane // 2) % 2 == core), 1)
    is_query = (row[:, :1] // 2) % 2 == core
    shape = (BLOCKS, QUERIES)
    piece = lax.broadcasted_iota(jnp.int32, shape, 1) // PIECE
    mine = (query_rank_down == piece) & is_query
    position = jnp.sum(jnp.where(mine, down[:, :1], 0), axis=0, keepdims=True)
    seen = []
    for group in range(N_GROUPS):
        last = position[:, (group + 1) * GROUP - 1 : (group + 1) * GROUP]
        seen.append(tally((across[:1] <= last) & (lane[:1] % 2 == half), 1))
    seen = jnp.concatenate(seen + [jnp.zeros((1, BLOCKS - N_GROUPS), jnp.int32)], axis=1)
    rest = jnp.zeros((5, BLOCKS), jnp.int32)
    meta[...] = jnp.concatenate([key_rank, query_rank, seen, rest], axis=0)
    offset = lax.broadcasted_iota(jnp.int32, (1, QUERIES), 1) % PIECE
    offset = offset + (lax.axis_index("y") // 2) * PIECE
    q_pos[...] = jnp.broadcast_to(position + offset, q_pos.shape)


def pack_kernel(
    block_start,
    kv_any,
    wk_any,
    wv_any,
    q_any,
    g_any,
    out_any,
    meta,
    q_pos,
    kv_ref,
    wk_ref,
    wv_ref,
    q_ref,
    g_ref,
    out_ref,
    sems,
    out_sems,
):
    pairs = [(q_any, q_ref), (g_any, g_ref), (kv_any, kv_ref), (wk_any, wk_ref), (wv_any, wv_ref)]
    copies = [
        pltpu.make_async_copy(source, target, sems.at[index])
        for index, (source, target) in enumerate(pairs)
    ]
    for copy in copies:
        copy.start()
    list_blocks(block_start, meta, q_pos)
    copies[0].wait()
    copies[1].wait()
    for x in range(HEADS):
        q_nope = q_ref[:, x * WIDTH_Q : x * WIDTH_Q + NOPE]
        q_rope = q_ref[:, x * WIDTH_Q + NOPE : (x + 1) * WIDTH_Q]
        grad = g_ref[:, x * VDIM : (x + 1) * VDIM]
        for y in range(SIDE):
            slot = y * SIDE + x
            first = slice((y // 2) * PIECE, (y // 2 + 1) * PIECE)
            second = slice(HALF + (y // 2) * PIECE, HALF + (y // 2 + 1) * PIECE)
            low = KEY_ROWS
            out_ref[slot, low : low + PIECE] = q_nope[first]
            out_ref[slot, low + PIECE : low + 2 * PIECE] = q_nope[second]
            out_ref[slot, low + 2 * PIECE : low + 3 * PIECE] = grad[first]
            out_ref[slot, low + 3 * PIECE : low + 4 * PIECE] = grad[second]
            out_ref[slot, low + 4 * PIECE : low + 5 * PIECE] = jnp.concatenate(
                [q_rope[first], q_rope[second]], axis=1
            )
    part = (slice(None), pl.ds(KEY_ROWS, IN_ROWS - KEY_ROWS))
    sent = [pltpu.make_async_copy(out_ref.at[part], out_any.at[part], out_sems.at[SIDE])]
    sent[0].start()
    copies[2].wait()
    values = kv_ref[:LATENT, :].astype(f32)
    inverse = lax.rsqrt(jnp.mean(values * values, axis=0, keepdims=True) + eps)
    normed = (values * inverse).T.astype(bf16)
    rope = kv_ref[LATENT:, :].astype(f32).T.astype(bf16)
    copies[3].wait()
    keys = dot(normed, wk_ref[...]).astype(bf16)
    copies[4].wait()
    values = dot(normed, wv_ref[...]).astype(bf16)
    for y in range(SIDE):
        low = (y % 2) * HALF
        for x in range(HEADS):
            slot = y * SIDE + x
            out_ref[slot, :HALF] = keys[low : low + HALF, x * NOPE : (x + 1) * NOPE]
            out_ref[slot, HALF : 2 * HALF] = values[low : low + HALF, x * VDIM : (x + 1) * VDIM]
            out_ref[slot, 2 * HALF : KEY_ROWS] = jnp.concatenate(
                [rope[low : low + PIECE], rope[low + PIECE : low + HALF]], axis=1
            )
        part = (pl.ds(y * SIDE, SIDE), pl.ds(0, KEY_ROWS))
        sent.append(pltpu.make_async_copy(out_ref.at[part], out_any.at[part], out_sems.at[y]))
        sent[-1].start()
    for copy in sent:
        copy.wait()


def key_block(chip, core):
    return (2 * chip + core) * 2 + lax.axis_index("y") % 2


def place_positions(block_start, meta, k_pos):
    rows = lax.broadcasted_iota(jnp.int32, (HALF, NOPE), 0)

    def body(index, carry):
        block = 2 * index + lax.axis_index("y") % 2
        at = pl.ds(pl.multiple_of(meta[0, block] * HALF, HALF), HALF)
        k_pos[at, :] = rows + block_start[block]
        return carry

    lax.fori_loop(0, 2 * CHIPS, body, 0, unroll=UNROLL)


def step_rows(group):
    return CHUNK // 2 if group == 0 else CHUNK


def seen_steps(meta, group):
    return (meta[2, group] * HALF + step_rows(group) - 1) // step_rows(group)


def place_kernel(block_start, meta, own_ref, queries, grads, k_pos):
    core = lax.axis_index("core")
    pad = jnp.zeros((PIECE, HALF), bf16)

    def place(chip, carry):
        low = KEY_ROWS
        q_rope = own_ref[chip, low + 4 * PIECE : low + 5 * PIECE]
        for half in range(2):
            rank = meta[1, (2 * chip + core) * 2 + half]
            at = pl.ds(pl.multiple_of(rank * PIECE, PIECE), PIECE)
            queries[at, :NOPE] = own_ref[chip, low + half * PIECE : low + (half + 1) * PIECE]
            queries[at, NOPE:] = jnp.concatenate(
                [q_rope[:, half * HALF : (half + 1) * HALF], pad], axis=1
            )
            grads[at, :] = own_ref[chip, low + (2 + half) * PIECE : low + (3 + half) * PIECE]
        return carry

    lax.fori_loop(0, CHIPS, place, 0, unroll=UNROLL)
    place_positions(block_start, meta, k_pos)


def stats_kernel(
    meta,
    q_pos,
    own_ref,
    other_ref,
    queries,
    grads,
    k_pos,
    keys,
    stats,
    scores,
    slopes,
    values,
):
    core = lax.axis_index("core")
    pad = jnp.zeros((HALF, HALF), bf16)

    def place(chip, carry):
        for ref, side in ((own_ref, core), (other_ref, 1 - core)):
            rank = meta[0, key_block(chip, side)]
            at = pl.ds(pl.multiple_of(rank * HALF, HALF), HALF)
            rope = ref[chip, 2 * HALF : KEY_ROWS]
            rope = jnp.concatenate([rope[:, :HALF], rope[:, HALF:]], axis=0)
            keys[at, :NOPE] = ref[chip, :HALF]
            keys[at, NOPE:] = jnp.concatenate([rope, pad], axis=1)
            values[at, :] = ref[chip, HALF : 2 * HALF]
        return carry

    lax.fori_loop(0, CHIPS, place, 0, unroll=UNROLL)

    for group in range(N_GROUPS):
        lanes = slice(group * GROUP, (group + 1) * GROUP)
        q_group = queries[lanes, :]
        g_group = grads[lanes, :]
        q_at = q_pos[0:1, lanes]

        rows = step_rows(group)

        def gather_stats(index, carry, lanes=lanes, rows=rows):
            top, weight_sum, weighted = carry
            at = pl.ds(pl.multiple_of(index * rows, rows), rows)
            score = dot(keys[at, :], q_group, 1, 1) * (SCALE * LOG2E)
            key_at = jnp.concatenate([k_pos[at, :]] * (GROUP // NOPE), axis=1)
            score = jnp.where(key_at <= q_at, score, masked_low)
            slope = dot(values[at, :], g_group, 1, 1)
            scores[at, lanes] = score
            slopes[at, lanes] = slope
            fresh = jnp.maximum(top, jnp.max(score, axis=0, keepdims=True))
            fade = jnp.exp2(top - fresh)
            weight = jnp.exp2(score - fresh)
            weight_sum = weight_sum * fade + jnp.sum(weight, axis=0, keepdims=True)
            weighted = weighted * fade + jnp.sum(weight * slope, axis=0, keepdims=True)
            return (fresh, weight_sum, weighted)

        zero = jnp.zeros((1, GROUP), f32)
        top, weight_sum, weighted = lax.fori_loop(
            0,
            seen_steps(meta, group),
            gather_stats,
            (jnp.full((1, GROUP), masked_low, f32), zero, zero),
        )
        stats[:, lanes] = jnp.concatenate(
            [top, weight_sum, weighted, jnp.zeros((5, GROUP), f32)], axis=0
        )


def gradient_kernel(
    meta,
    keys,
    queries,
    grads,
    scores,
    slopes,
    own_stats,
    other_stats,
    own_out,
    other_out,
    key_grads,
    value_grads,
    query_grads,
    key_sum,
    value_sum,
):
    own_top = own_stats[0:1, :]
    other_top = other_stats[0:1, :]
    top = jnp.maximum(own_top, other_top)
    own_fade = jnp.exp2(own_top - top)
    other_fade = jnp.exp2(other_top - top)
    weight_sum = own_stats[1:2, :] * own_fade + other_stats[1:2, :] * other_fade
    weighted = own_stats[2:3, :] * own_fade + other_stats[2:3, :] * other_fade
    log_total = top + jnp.log2(weight_sum)
    average = weighted / weight_sum
    query_grads[...] = jnp.zeros_like(query_grads)

    def gradients(index, carry):
        at = pl.ds(pl.multiple_of(index * CHUNK, CHUNK), CHUNK)
        key_sum[...] = jnp.zeros_like(key_sum)
        value_sum[...] = jnp.zeros_like(value_sum)
        for group in range(N_GROUPS):
            lanes = slice(group * GROUP, (group + 1) * GROUP)
            rows = step_rows(group)
            for step in range(CHUNK // rows):

                @pl.when(index * (CHUNK // rows) + step < seen_steps(meta, group))
                def _(lanes=lanes, rows=rows, step=step):
                    part = slice(step * rows, (step + 1) * rows)
                    at = pl.ds(pl.multiple_of(index * CHUNK + step * rows, rows), rows)
                    probs = jnp.exp2(scores[at, lanes] - log_total[:, lanes])
                    slope = (slopes[at, lanes] - average[:, lanes]) * SCALE
                    score_grad = (probs * slope).astype(bf16)
                    value_sum[part, :] += dot(probs.astype(bf16), grads[lanes, :])
                    key_sum[part, :] += dot(score_grad, queries[lanes, :])
                    query_grads[lanes, :] += dot(score_grad, keys[at, :], 0, 0)

        key_grads[at, :] = key_sum[...].astype(bf16)
        value_grads[at, :] = value_sum[...].astype(bf16)
        return carry

    lax.fori_loop(0, N_CHUNKS, gradients, 0)
    core = lax.axis_index("core")

    def hand_out(chip, carry):
        for ref, side in ((own_out, core), (other_out, 1 - core)):
            rank = meta[0, key_block(chip, side)]
            at = pl.ds(pl.multiple_of(rank * HALF, HALF), HALF)
            ref[chip, :HALF] = key_grads[at, :NOPE]
            ref[chip, HALF : 2 * HALF] = value_grads[at, :]
            rope = key_grads[at, NOPE:WIDTH_Q]
            ref[chip, 2 * HALF : KEY_ROWS] = jnp.concatenate([rope[:PIECE], rope[PIECE:]], axis=1)
        low = KEY_ROWS
        ropes = []
        for half in range(2):
            rank = meta[1, (2 * chip + core) * 2 + half]
            at = pl.ds(pl.multiple_of(rank * PIECE, PIECE), PIECE)
            piece = query_grads[at, :].astype(bf16)
            own_out[chip, low + half * PIECE : low + (half + 1) * PIECE] = piece[:, :NOPE]
            ropes.append(piece[:, NOPE:WIDTH_Q])
        own_out[chip, low + 2 * PIECE : low + 3 * PIECE] = jnp.concatenate(ropes, axis=1)
        return carry

    lax.fori_loop(0, CHIPS, hand_out, 0, unroll=UNROLL)


def slot_sum(slots_ref, slots, low, rows):
    total = slots_ref[slots[0], low : low + rows].astype(f32)
    for slot in slots[1:]:
        total = total + slots_ref[slot, low : low + rows].astype(f32)
    return total


def head_sums(slots_ref, low):
    parts = []
    for x in range(HEADS):
        halves = [
            slot_sum(slots_ref, (y * SIDE + x, (y + 2) * SIDE + x), low, HALF) for y in range(2)
        ]
        parts.append(jnp.concatenate(halves, axis=0).astype(bf16))
    return jnp.concatenate(parts, axis=1)


def latent_kernel(
    slots_ref, wk_ref, wv_ref, kv_ref, out_ref, grad_q_ref, own_ref, other_ref, terms
):
    key_flat = head_sums(slots_ref, 0)
    value_flat = head_sums(slots_ref, HALF)
    latent = dot(key_flat, wk_ref[...], 1, 1) + dot(value_flat, wv_ref[...], 1, 1)
    out_ref[:, :LATENT] = latent.astype(bf16)
    ropes = []
    for y in range(2):
        slots = [row * SIDE + x for row in (y, y + 2) for x in range(HEADS)]
        rope = slot_sum(slots_ref, slots, 2 * HALF, PIECE)
        ropes += [rope[:, :HALF], rope[:, HALF:]]
    rope = jnp.concatenate(ropes, axis=0)
    out_ref[:, LATENT:] = jnp.concatenate([rope, jnp.zeros_like(rope)], axis=1).astype(bf16)
    values = kv_ref[:LATENT, :].astype(f32)
    inverse = lax.rsqrt(jnp.mean(values * values, axis=0, keepdims=True) + eps)
    normed = (values * inverse).astype(bf16)
    terms[:, : HEADS * NOPE] = dot(normed, key_flat).astype(bf16)
    terms[:, HEADS * NOPE :] = dot(normed, value_flat).astype(bf16)
    core = lax.axis_index("core")
    y_here, x_here = lax.axis_index("y"), lax.axis_index("x")
    for dx in range(SIDE):
        for dy in range(SIDE):
            chip = (y_here ^ dy) * SIDE + (x_here ^ dx)
            first = pl.multiple_of((2 * chip + core) * W_ROWS, W_ROWS)
            second = pl.multiple_of((2 * chip + 1 - core) * W_ROWS, W_ROWS)
            own_ref[dx, dy] = terms[pl.ds(first, W_ROWS), :]
            other_ref[dx, dy] = terms[pl.ds(second, W_ROWS), :]
    low = KEY_ROWS
    for quarter in range(2):
        for half in range(2):
            parts = []
            for x in range(HEADS):
                slots = (2 * quarter * SIDE + x, (2 * quarter + 1) * SIDE + x)
                parts.append(slot_sum(slots_ref, slots, low + half * PIECE, PIECE))
                rope = slot_sum(slots_ref, slots, low + 2 * PIECE, PIECE)
                parts.append(rope[:, half * HALF : (half + 1) * HALF])
            first = half * HALF + quarter * PIECE
            grad_q_ref[first : first + PIECE, :] = jnp.concatenate(parts, axis=1).astype(bf16)


def norm_kernel(slots_ref, kv_ref, out_ref):
    total = jnp.sum(slots_ref[...].astype(f32), axis=0)
    x_hat, inverse = rms_rows(kv_ref[:, :LATENT])
    latent = total[:, :LATENT]
    latent = inverse * (latent - x_hat * jnp.mean(latent * x_hat, axis=-1, keepdims=True))
    row = jnp.concatenate([latent, total[:, LATENT:]], axis=1).astype(bf16)
    out_ref[...] = jnp.broadcast_to(row[None], out_ref.shape)


def call(kernel, shapes, specs, scratch=(), limit=32, flops=0, moved=0, out_specs=None):
    shapes = [jax.ShapeDtypeStruct(*shape) for shape in shapes]
    single = len(shapes) == 1
    if out_specs is None:
        out_specs = VMEM if single else [VMEM] * len(shapes)
    return pl.pallas_call(
        kernel,
        out_shape=shapes[0] if single else shapes,
        in_specs=specs,
        out_specs=out_specs,
        scratch_shapes=scratch,
        compiler_params=pltpu.CompilerParams(vmem_limit_bytes=limit * 2**20),
        cost_estimate=pl.CostEstimate(flops=flops, bytes_accessed=moved, transcendentals=0),
    )


def run_pack(*args):
    return call(
        pack_kernel,
        [
            ((CHIPS, IN_ROWS, NOPE), bf16),
            ((8, BLOCKS), jnp.int32),
            ((8, QUERIES), jnp.int32),
        ],
        [VMEM] + [ANY] * 5,
        [
            pltpu.VMEM((LATENT + ROPE, ROWS), bf16),
            pltpu.VMEM((LATENT, HEADS * NOPE), bf16),
            pltpu.VMEM((LATENT, HEADS * VDIM), bf16),
            pltpu.VMEM((ROWS, HEADS * WIDTH_Q), bf16),
            pltpu.VMEM((ROWS, HEADS * VDIM), bf16),
            pltpu.VMEM((CHIPS, IN_ROWS, NOPE), bf16),
            pltpu.SemaphoreType.DMA((5,)),
            pltpu.SemaphoreType.DMA((SIDE + 1,)),
        ],
        limit=60,
        out_specs=[ANY, VMEM, VMEM],
    )(*args)


def run_place(*args):
    return call(
        place_kernel,
        [((QUERIES, 2 * NOPE), bf16), ((QUERIES, VDIM), bf16), ((KEYS, NOPE), jnp.int32)],
        [SMEM] * 2 + [VMEM],
        limit=16,
        flops=10**8,
        moved=4 * 2**20,
    )(*args)


def run_stats(*args):
    return call(
        stats_kernel,
        [
            ((KEYS, 2 * NOPE), bf16),
            ((8, QUERIES), f32),
            ((KEYS, QUERIES), f32),
            ((KEYS, QUERIES), f32),
        ],
        [SMEM] + [VMEM] * 6,
        [pltpu.VMEM((KEYS, VDIM), bf16)],
        limit=28,
    )(*args)


def run_gradient(*args):
    return call(
        gradient_kernel,
        [((CHIPS, OUT_ROWS, NOPE), bf16), ((CHIPS, KEY_ROWS, NOPE), bf16)],
        [SMEM] + [VMEM] * 7,
        [
            pltpu.VMEM((KEYS, 2 * NOPE), bf16),
            pltpu.VMEM((KEYS, VDIM), bf16),
            pltpu.VMEM((QUERIES, 2 * NOPE), f32),
            pltpu.VMEM((CHUNK, 2 * NOPE), f32),
            pltpu.VMEM((CHUNK, VDIM), f32),
        ],
        limit=28,
    )(*args)


def over_chips(slots):
    return lax.all_to_all(slots, ("y", "x"), 0, 0)


def swap(array, axis, bit):
    return lax.ppermute(array, axis, [(i, i ^ bit) for i in range(lax.axis_size(axis))])


def local(query, kv_row, w_uk, w_uv, grad_out, block_start):
    z_size = lax.axis_size("head")
    z_rows = ROWS // z_size
    kv_t = kv_row.T
    slots, meta, q_pos = run_pack(
        block_start.reshape(1, BLOCKS), kv_t, w_uk, w_uv, query, grad_out
    )
    own = over_chips(slots)
    other = swap(own[:, :KEY_ROWS], "core", 1)

    queries, grads, k_pos = run_place(block_start, meta, own)
    keys, stats, scores, slopes = run_stats(meta, q_pos, own, other, queries, grads, k_pos)
    own_part, other_part = run_gradient(
        meta, keys, queries, grads, scores, slopes, stats, swap(stats, "y", 1)
    )
    slots = over_chips(own_part.at[:, :KEY_ROWS].add(swap(other_part, "core", 1)))

    z_part, grad_query, own_terms, other_terms = call(
        latent_kernel,
        [((ROWS, Z_WIDTH), bf16), ((ROWS, HEADS * WIDTH_Q), bf16)]
        + [((SIDE, SIDE, W_ROWS, W_WIDTH), bf16)] * 2,
        [VMEM] * 4,
        [pltpu.VMEM((LATENT, W_WIDTH), bf16)],
    )(slots, w_uk, w_uv, kv_t)
    terms = own_terms + swap(other_terms, "core", 1)
    for axis in ("x", "y"):
        total = terms[0].astype(f32)
        for bit in (3, 2, 1):
            total = total + swap(terms[bit], axis, bit).astype(f32)
        terms = total.astype(bf16)

    z_slots = lax.all_to_all(z_part.reshape(z_size, z_rows, Z_WIDTH), "head", 0, 0)
    first_row = lax.axis_index("head") * z_rows
    kv_rows = lax.dynamic_slice_in_dim(kv_row, first_row, z_rows)
    rows = call(norm_kernel, [((z_size, z_rows, Z_WIDTH), bf16)], [VMEM] * 2)(z_slots, kv_rows)
    all_rows = lax.all_to_all(rows, "head", 0, 0).reshape(ROWS, Z_WIDTH)
    grad_kv_row = all_rows[:, : LATENT + ROPE].astype(f32)
    width = HEADS * NOPE
    return (grad_query, grad_kv_row, total[:, :width], total[:, width:])


def solution(mesh):
    axes = ("y", "x", "core")
    devices = mesh.devices.reshape(SIDE, SIDE, 2, mesh.shape["head"])
    placed = (
        P(axes, "head"),
        P(axes, None),
        P(None, "head"),
        P(None, "head"),
        P(axes, "head"),
        P(),
    )
    return jax.shard_map(
        local,
        mesh=Mesh(devices, (*axes, "head")),
        in_specs=placed,
        out_specs=(P(axes, "head"), P(axes, None), P(axes, "head"), P(axes, "head")),
        check_vma=False,
    )
```

```python
import math

import jax
import jax.numpy as jnp
from jax import lax
from jax.experimental import pallas as pl
from jax.experimental.pallas import tpu as pltpu
from jax.sharding import Mesh
from jax.sharding import PartitionSpec as P

LATENT = 512
ROPE = 64
NOPE = 128
VDIM = 128
WIDTH_Q = NOPE + ROPE
HALF = 64
BLOCKS = 64
HEADS = 4
SIDE = 4
CHIPS = SIDE * SIDE
PIECE = HALF // 2
ROWS = 2 * HALF
KEYS = 2 * CHIPS * HALF
QUERIES = 2 * CHIPS * PIECE
KEY_ROWS = 2 * HALF + PIECE
IN_ROWS = KEY_ROWS + 5 * PIECE
OUT_ROWS = KEY_ROWS + 3 * PIECE
W_ROWS = LATENT // (2 * CHIPS)
W_WIDTH = HEADS * (NOPE + VDIM)
CHUNK = 1024
GROUP = 512
N_CHUNKS = KEYS // CHUNK
N_GROUPS = QUERIES // GROUP
UNROLL = CHIPS
Z_WIDTH = 640
LOG2E = 1.4426950408889634
SCALE = 1.0 / math.sqrt(WIDTH_Q)

eps = 1e-06
masked_low = -1e30
bf16 = jnp.bfloat16
f32 = jnp.float32
VMEM = pl.BlockSpec(memory_space=pltpu.VMEM)
SMEM = pl.BlockSpec(memory_space=pltpu.SMEM)
ANY = pl.BlockSpec(memory_space=pl.ANY)


def dot(left, right, left_dim=1, right_dim=0):
    return lax.dot_general(
        left, right, (((left_dim,), (right_dim,)), ((), ())), preferred_element_type=f32
    )


def rms_rows(latent):
    values = latent.astype(f32)
    inverse = lax.rsqrt(jnp.mean(values * values, axis=-1, keepdims=True) + eps)
    return (values * inverse, inverse)


def list_blocks(starts, meta, q_pos):
    half = lax.axis_index("y") % 2
    core = lax.axis_index("core")
    shape = (BLOCKS, BLOCKS)
    across = jnp.broadcast_to(starts[...], shape)
    down = across.T
    row = lax.broadcasted_iota(jnp.int32, shape, 0)
    lane = lax.broadcasted_iota(jnp.int32, shape, 1)

    def tally(where, axis):
        return jnp.sum(where.astype(jnp.int32), axis=axis, keepdims=True)

    key_rank = tally((down < across) & (row % 2 == half), 0)
    query_rank = tally((down < across) & ((row // 2) % 2 == core), 0)
    query_rank_down = tally((across < down) & ((lane // 2) % 2 == core), 1)
    is_query = (row[:, :1] // 2) % 2 == core
    shape = (BLOCKS, QUERIES)
    piece = lax.broadcasted_iota(jnp.int32, shape, 1) // PIECE
    mine = (query_rank_down == piece) & is_query
    position = jnp.sum(jnp.where(mine, down[:, :1], 0), axis=0, keepdims=True)
    seen = []
    for group in range(N_GROUPS):
        last = position[:, (group + 1) * GROUP - 1 : (group + 1) * GROUP]
        seen.append(tally((across[:1] <= last) & (lane[:1] % 2 == half), 1))
    seen = jnp.concatenate(seen + [jnp.zeros((1, BLOCKS - N_GROUPS), jnp.int32)], axis=1)
    rest = jnp.zeros((5, BLOCKS), jnp.int32)
    meta[...] = jnp.concatenate([key_rank, query_rank, seen, rest], axis=0)
    offset = lax.broadcasted_iota(jnp.int32, (1, QUERIES), 1) % PIECE
    offset = offset + (lax.axis_index("y") // 2) * PIECE
    q_pos[...] = jnp.broadcast_to(position + offset, q_pos.shape)


def pack_kernel(
    block_start,
    kv_any,
    wk_any,
    wv_any,
    q_any,
    g_any,
    out_any,
    meta,
    q_pos,
    kv_ref,
    wk_ref,
    wv_ref,
    q_ref,
    g_ref,
    out_ref,
    sems,
    out_sems,
):
    pairs = [(q_any, q_ref), (g_any, g_ref), (kv_any, kv_ref), (wk_any, wk_ref), (wv_any, wv_ref)]
    copies = [
        pltpu.make_async_copy(source, target, sems.at[index])
        for index, (source, target) in enumerate(pairs)
    ]
    for copy in copies:
        copy.start()
    list_blocks(block_start, meta, q_pos)
    copies[0].wait()
    copies[1].wait()
    for x in range(HEADS):
        q_nope = q_ref[:, x * WIDTH_Q : x * WIDTH_Q + NOPE]
        q_rope = q_ref[:, x * WIDTH_Q + NOPE : (x + 1) * WIDTH_Q]
        grad = g_ref[:, x * VDIM : (x + 1) * VDIM]
        for y in range(SIDE):
            slot = y * SIDE + x
            first = slice((y // 2) * PIECE, (y // 2 + 1) * PIECE)
            second = slice(HALF + (y // 2) * PIECE, HALF + (y // 2 + 1) * PIECE)
            low = KEY_ROWS
            out_ref[slot, low : low + PIECE] = q_nope[first]
            out_ref[slot, low + PIECE : low + 2 * PIECE] = q_nope[second]
            out_ref[slot, low + 2 * PIECE : low + 3 * PIECE] = grad[first]
            out_ref[slot, low + 3 * PIECE : low + 4 * PIECE] = grad[second]
            out_ref[slot, low + 4 * PIECE : low + 5 * PIECE] = jnp.concatenate(
                [q_rope[first], q_rope[second]], axis=1
            )
    part = (slice(None), pl.ds(KEY_ROWS, IN_ROWS - KEY_ROWS))
    sent = [pltpu.make_async_copy(out_ref.at[part], out_any.at[part], out_sems.at[SIDE])]
    sent[0].start()
    copies[2].wait()
    values = kv_ref[:LATENT, :].astype(f32)
    inverse = lax.rsqrt(jnp.mean(values * values, axis=0, keepdims=True) + eps)
    normed = (values * inverse).T.astype(bf16)
    rope = kv_ref[LATENT:, :].astype(f32).T.astype(bf16)
    copies[3].wait()
    keys = dot(normed, wk_ref[...]).astype(bf16)
    copies[4].wait()
    values = dot(normed, wv_ref[...]).astype(bf16)
    for y in range(SIDE):
        low = (y % 2) * HALF
        for x in range(HEADS):
            slot = y * SIDE + x
            out_ref[slot, :HALF] = keys[low : low + HALF, x * NOPE : (x + 1) * NOPE]
            out_ref[slot, HALF : 2 * HALF] = values[low : low + HALF, x * VDIM : (x + 1) * VDIM]
            out_ref[slot, 2 * HALF : KEY_ROWS] = jnp.concatenate(
                [rope[low : low + PIECE], rope[low + PIECE : low + HALF]], axis=1
            )
        part = (pl.ds(y * SIDE, SIDE), pl.ds(0, KEY_ROWS))
        sent.append(pltpu.make_async_copy(out_ref.at[part], out_any.at[part], out_sems.at[y]))
        sent[-1].start()
    for copy in sent:
        copy.wait()


def key_block(chip, core):
    return (2 * chip + core) * 2 + lax.axis_index("y") % 2


def place_positions(block_start, meta, k_pos):
    rows = lax.broadcasted_iota(jnp.int32, (HALF, NOPE), 0)

    def body(index, carry):
        block = 2 * index + lax.axis_index("y") % 2
        at = pl.ds(pl.multiple_of(meta[0, block] * HALF, HALF), HALF)
        k_pos[at, :] = rows + block_start[block]
        return carry

    lax.fori_loop(0, 2 * CHIPS, body, 0, unroll=UNROLL)


def step_rows(group):
    return CHUNK // 2 if group == 0 else CHUNK


def seen_steps(meta, group):
    return (meta[2, group] * HALF + step_rows(group) - 1) // step_rows(group)


def place_kernel(block_start, meta, own_ref, queries, grads, k_pos):
    core = lax.axis_index("core")
    pad = jnp.zeros((PIECE, HALF), bf16)

    def place(chip, carry):
        low = KEY_ROWS
        q_rope = own_ref[chip, low + 4 * PIECE : low + 5 * PIECE]
        for half in range(2):
            rank = meta[1, (2 * chip + core) * 2 + half]
            at = pl.ds(pl.multiple_of(rank * PIECE, PIECE), PIECE)
            queries[at, :NOPE] = own_ref[chip, low + half * PIECE : low + (half + 1) * PIECE]
            queries[at, NOPE:] = jnp.concatenate(
                [q_rope[:, half * HALF : (half + 1) * HALF], pad], axis=1
            )
            grads[at, :] = own_ref[chip, low + (2 + half) * PIECE : low + (3 + half) * PIECE]
        return carry

    lax.fori_loop(0, CHIPS, place, 0, unroll=UNROLL)
    place_positions(block_start, meta, k_pos)


def stats_kernel(
    meta,
    q_pos,
    own_ref,
    other_ref,
    queries,
    grads,
    k_pos,
    keys,
    stats,
    scores,
    slopes,
    values,
):
    core = lax.axis_index("core")
    pad = jnp.zeros((HALF, HALF), bf16)

    def place(chip, carry):
        for ref, side in ((own_ref, core), (other_ref, 1 - core)):
            rank = meta[0, key_block(chip, side)]
            at = pl.ds(pl.multiple_of(rank * HALF, HALF), HALF)
            rope = ref[chip, 2 * HALF : KEY_ROWS]
            rope = jnp.concatenate([rope[:, :HALF], rope[:, HALF:]], axis=0)
            keys[at, :NOPE] = ref[chip, :HALF]
            keys[at, NOPE:] = jnp.concatenate([rope, pad], axis=1)
            values[at, :] = ref[chip, HALF : 2 * HALF]
        return carry

    lax.fori_loop(0, CHIPS, place, 0, unroll=UNROLL)

    for group in range(N_GROUPS):
        lanes = slice(group * GROUP, (group + 1) * GROUP)
        q_group = queries[lanes, :]
        g_group = grads[lanes, :]
        q_at = q_pos[0:1, lanes]

        rows = step_rows(group)

        def gather_stats(index, carry, lanes=lanes, rows=rows):
            top, weight_sum, weighted = carry
            at = pl.ds(pl.multiple_of(index * rows, rows), rows)
            score = dot(keys[at, :], q_group, 1, 1) * (SCALE * LOG2E)
            key_at = jnp.concatenate([k_pos[at, :]] * (GROUP // NOPE), axis=1)
            score = jnp.where(key_at <= q_at, score, masked_low)
            slope = dot(values[at, :], g_group, 1, 1)
            scores[at, lanes] = score
            slopes[at, lanes] = slope
            fresh = jnp.maximum(top, jnp.max(score, axis=0, keepdims=True))
            fade = jnp.exp2(top - fresh)
            weight = jnp.exp2(score - fresh)
            weight_sum = weight_sum * fade + jnp.sum(weight, axis=0, keepdims=True)
            weighted = weighted * fade + jnp.sum(weight * slope, axis=0, keepdims=True)
            return (fresh, weight_sum, weighted)

        zero = jnp.zeros((1, GROUP), f32)
        top, weight_sum, weighted = lax.fori_loop(
            0,
            seen_steps(meta, group),
            gather_stats,
            (jnp.full((1, GROUP), masked_low, f32), zero, zero),
        )
        stats[:, lanes] = jnp.concatenate(
            [top, weight_sum, weighted, jnp.zeros((5, GROUP), f32)], axis=0
        )


def gradient_kernel(
    meta,
    keys,
    queries,
    grads,
    scores,
    slopes,
    own_stats,
    other_stats,
    own_out,
    other_out,
    key_grads,
    value_grads,
    query_grads,
    key_sum,
    value_sum,
):
    own_top = own_stats[0:1, :]
    other_top = other_stats[0:1, :]
    top = jnp.maximum(own_top, other_top)
    own_fade = jnp.exp2(own_top - top)
    other_fade = jnp.exp2(other_top - top)
    weight_sum = own_stats[1:2, :] * own_fade + other_stats[1:2, :] * other_fade
    weighted = own_stats[2:3, :] * own_fade + other_stats[2:3, :] * other_fade
    log_scaled = top + jnp.log2(weight_sum) - math.log2(SCALE)
    average = weighted / weight_sum
    query_grads[...] = jnp.zeros_like(query_grads)

    def gradients(index, carry):
        at = pl.ds(pl.multiple_of(index * CHUNK, CHUNK), CHUNK)
        key_sum[...] = jnp.zeros_like(key_sum)
        value_sum[...] = jnp.zeros_like(value_sum)
        for group in range(N_GROUPS):
            lanes = slice(group * GROUP, (group + 1) * GROUP)
            rows = step_rows(group)
            for step in range(CHUNK // rows):

                @pl.when(index * (CHUNK // rows) + step < seen_steps(meta, group))
                def _(lanes=lanes, rows=rows, step=step):
                    part = slice(step * rows, (step + 1) * rows)
                    at = pl.ds(pl.multiple_of(index * CHUNK + step * rows, rows), rows)
                    probs = jnp.exp2(scores[at, lanes] - log_scaled[:, lanes])
                    score_grad = (probs * (slopes[at, lanes] - average[:, lanes])).astype(bf16)
                    value_sum[part, :] += dot(probs.astype(bf16), grads[lanes, :])
                    key_sum[part, :] += dot(score_grad, queries[lanes, :])
                    query_grads[lanes, :] += dot(score_grad, keys[at, :], 0, 0)

        key_grads[at, :] = key_sum[...].astype(bf16)
        value_grads[at, :] = (value_sum[...] * (1.0 / SCALE)).astype(bf16)
        return carry

    lax.fori_loop(0, N_CHUNKS, gradients, 0)
    core = lax.axis_index("core")

    def hand_out(chip, carry):
        for ref, side in ((own_out, core), (other_out, 1 - core)):
            rank = meta[0, key_block(chip, side)]
            at = pl.ds(pl.multiple_of(rank * HALF, HALF), HALF)
            ref[chip, :HALF] = key_grads[at, :NOPE]
            ref[chip, HALF : 2 * HALF] = value_grads[at, :]
            rope = key_grads[at, NOPE:WIDTH_Q]
            ref[chip, 2 * HALF : KEY_ROWS] = jnp.concatenate([rope[:PIECE], rope[PIECE:]], axis=1)
        low = KEY_ROWS
        ropes = []
        for half in range(2):
            rank = meta[1, (2 * chip + core) * 2 + half]
            at = pl.ds(pl.multiple_of(rank * PIECE, PIECE), PIECE)
            piece = query_grads[at, :].astype(bf16)
            own_out[chip, low + half * PIECE : low + (half + 1) * PIECE] = piece[:, :NOPE]
            ropes.append(piece[:, NOPE:WIDTH_Q])
        own_out[chip, low + 2 * PIECE : low + 3 * PIECE] = jnp.concatenate(ropes, axis=1)
        return carry

    lax.fori_loop(0, CHIPS, hand_out, 0, unroll=UNROLL)


def slot_sum(slots_ref, slots, low, rows):
    total = slots_ref[slots[0], low : low + rows].astype(f32)
    for slot in slots[1:]:
        total = total + slots_ref[slot, low : low + rows].astype(f32)
    return total


def head_sums(slots_ref, low):
    parts = []
    for x in range(HEADS):
        halves = [
            slot_sum(slots_ref, (y * SIDE + x, (y + 2) * SIDE + x), low, HALF) for y in range(2)
        ]
        parts.append(jnp.concatenate(halves, axis=0).astype(bf16))
    return jnp.concatenate(parts, axis=1)


def latent_kernel(
    slots_ref, wk_ref, wv_ref, kv_ref, out_ref, grad_q_ref, own_ref, other_ref, terms
):
    key_flat = head_sums(slots_ref, 0)
    value_flat = head_sums(slots_ref, HALF)
    latent = dot(key_flat, wk_ref[...], 1, 1) + dot(value_flat, wv_ref[...], 1, 1)
    out_ref[:, :LATENT] = latent.astype(bf16)
    ropes = []
    for y in range(2):
        slots = [row * SIDE + x for row in (y, y + 2) for x in range(HEADS)]
        rope = slot_sum(slots_ref, slots, 2 * HALF, PIECE)
        ropes += [rope[:, :HALF], rope[:, HALF:]]
    rope = jnp.concatenate(ropes, axis=0)
    out_ref[:, LATENT:] = jnp.concatenate([rope, jnp.zeros_like(rope)], axis=1).astype(bf16)
    values = kv_ref[:LATENT, :].astype(f32)
    inverse = lax.rsqrt(jnp.mean(values * values, axis=0, keepdims=True) + eps)
    normed = (values * inverse).astype(bf16)
    terms[:, : HEADS * NOPE] = dot(normed, key_flat).astype(bf16)
    terms[:, HEADS * NOPE :] = dot(normed, value_flat).astype(bf16)
    core = lax.axis_index("core")
    y_here, x_here = lax.axis_index("y"), lax.axis_index("x")
    for dx in range(SIDE):
        for dy in range(SIDE):
            chip = (y_here ^ dy) * SIDE + (x_here ^ dx)
            first = pl.multiple_of((2 * chip + core) * W_ROWS, W_ROWS)
            second = pl.multiple_of((2 * chip + 1 - core) * W_ROWS, W_ROWS)
            own_ref[dx, dy] = terms[pl.ds(first, W_ROWS), :]
            other_ref[dx, dy] = terms[pl.ds(second, W_ROWS), :]
    low = KEY_ROWS
    for quarter in range(2):
        for half in range(2):
            parts = []
            for x in range(HEADS):
                slots = (2 * quarter * SIDE + x, (2 * quarter + 1) * SIDE + x)
                parts.append(slot_sum(slots_ref, slots, low + half * PIECE, PIECE))
                rope = slot_sum(slots_ref, slots, low + 2 * PIECE, PIECE)
                parts.append(rope[:, half * HALF : (half + 1) * HALF])
            first = half * HALF + quarter * PIECE
            grad_q_ref[first : first + PIECE, :] = jnp.concatenate(parts, axis=1).astype(bf16)


def norm_kernel(slots_ref, kv_ref, out_ref):
    total = jnp.sum(slots_ref[...].astype(f32), axis=0)
    x_hat, inverse = rms_rows(kv_ref[:, :LATENT])
    latent = total[:, :LATENT]
    latent = inverse * (latent - x_hat * jnp.mean(latent * x_hat, axis=-1, keepdims=True))
    row = jnp.concatenate([latent, total[:, LATENT:]], axis=1).astype(bf16)
    out_ref[...] = jnp.broadcast_to(row[None], out_ref.shape)


def call(kernel, shapes, specs, scratch=(), limit=32, flops=0, moved=0, out_specs=None):
    shapes = [jax.ShapeDtypeStruct(*shape) for shape in shapes]
    single = len(shapes) == 1
    if out_specs is None:
        out_specs = VMEM if single else [VMEM] * len(shapes)
    return pl.pallas_call(
        kernel,
        out_shape=shapes[0] if single else shapes,
        in_specs=specs,
        out_specs=out_specs,
        scratch_shapes=scratch,
        compiler_params=pltpu.CompilerParams(vmem_limit_bytes=limit * 2**20),
        cost_estimate=pl.CostEstimate(flops=flops, bytes_accessed=moved, transcendentals=0),
    )


def run_pack(*args):
    return call(
        pack_kernel,
        [
            ((CHIPS, IN_ROWS, NOPE), bf16),
            ((8, BLOCKS), jnp.int32),
            ((8, QUERIES), jnp.int32),
        ],
        [VMEM] + [ANY] * 5,
        [
            pltpu.VMEM((LATENT + ROPE, ROWS), bf16),
            pltpu.VMEM((LATENT, HEADS * NOPE), bf16),
            pltpu.VMEM((LATENT, HEADS * VDIM), bf16),
            pltpu.VMEM((ROWS, HEADS * WIDTH_Q), bf16),
            pltpu.VMEM((ROWS, HEADS * VDIM), bf16),
            pltpu.VMEM((CHIPS, IN_ROWS, NOPE), bf16),
            pltpu.SemaphoreType.DMA((5,)),
            pltpu.SemaphoreType.DMA((SIDE + 1,)),
        ],
        limit=60,
        out_specs=[ANY, VMEM, VMEM],
    )(*args)


def run_place(*args):
    return call(
        place_kernel,
        [((QUERIES, 2 * NOPE), bf16), ((QUERIES, VDIM), bf16), ((KEYS, NOPE), jnp.int32)],
        [SMEM] * 2 + [VMEM],
        limit=16,
        flops=10**8,
        moved=4 * 2**20,
    )(*args)


def run_stats(*args):
    return call(
        stats_kernel,
        [
            ((KEYS, 2 * NOPE), bf16),
            ((8, QUERIES), f32),
            ((KEYS, QUERIES), f32),
            ((KEYS, QUERIES), f32),
        ],
        [SMEM] + [VMEM] * 6,
        [pltpu.VMEM((KEYS, VDIM), bf16)],
        limit=28,
    )(*args)


def run_gradient(*args):
    return call(
        gradient_kernel,
        [((CHIPS, OUT_ROWS, NOPE), bf16), ((CHIPS, KEY_ROWS, NOPE), bf16)],
        [SMEM] + [VMEM] * 7,
        [
            pltpu.VMEM((KEYS, 2 * NOPE), bf16),
            pltpu.VMEM((KEYS, VDIM), bf16),
            pltpu.VMEM((QUERIES, 2 * NOPE), f32),
            pltpu.VMEM((CHUNK, 2 * NOPE), f32),
            pltpu.VMEM((CHUNK, VDIM), f32),
        ],
        limit=28,
    )(*args)


def over_chips(slots):
    return lax.all_to_all(slots, ("y", "x"), 0, 0)


def swap(array, axis, bit):
    return lax.ppermute(array, axis, [(i, i ^ bit) for i in range(lax.axis_size(axis))])


def local(query, kv_row, w_uk, w_uv, grad_out, block_start):
    z_size = lax.axis_size("head")
    z_rows = ROWS // z_size
    kv_t = kv_row.T
    slots, meta, q_pos = run_pack(
        block_start.reshape(1, BLOCKS), kv_t, w_uk, w_uv, query, grad_out
    )
    own = over_chips(slots)
    other = swap(own[:, :KEY_ROWS], "core", 1)

    queries, grads, k_pos = run_place(block_start, meta, own)
    keys, stats, scores, slopes = run_stats(meta, q_pos, own, other, queries, grads, k_pos)
    own_part, other_part = run_gradient(
        meta, keys, queries, grads, scores, slopes, stats, swap(stats, "y", 1)
    )
    slots = over_chips(own_part.at[:, :KEY_ROWS].add(swap(other_part, "core", 1)))

    z_part, grad_query, own_terms, other_terms = call(
        latent_kernel,
        [((ROWS, Z_WIDTH), bf16), ((ROWS, HEADS * WIDTH_Q), bf16)]
        + [((SIDE, SIDE, W_ROWS, W_WIDTH), bf16)] * 2,
        [VMEM] * 4,
        [pltpu.VMEM((LATENT, W_WIDTH), bf16)],
    )(slots, w_uk, w_uv, kv_t)
    terms = own_terms + swap(other_terms, "core", 1)
    for axis in ("x", "y"):
        total = terms[0].astype(f32)
        for bit in (3, 2, 1):
            total = total + swap(terms[bit], axis, bit).astype(f32)
        terms = total.astype(bf16)

    z_slots = lax.all_to_all(z_part.reshape(z_size, z_rows, Z_WIDTH), "head", 0, 0)
    first_row = lax.axis_index("head") * z_rows
    kv_rows = lax.dynamic_slice_in_dim(kv_row, first_row, z_rows)
    rows = call(norm_kernel, [((z_size, z_rows, Z_WIDTH), bf16)], [VMEM] * 2)(z_slots, kv_rows)
    all_rows = lax.all_to_all(rows, "head", 0, 0).reshape(ROWS, Z_WIDTH)
    grad_kv_row = all_rows[:, : LATENT + ROPE].astype(f32)
    width = HEADS * NOPE
    return (grad_query, grad_kv_row, total[:, :width], total[:, width:])


def solution(mesh):
    axes = ("y", "x", "core")
    devices = mesh.devices.reshape(SIDE, SIDE, 2, mesh.shape["head"])
    placed = (
        P(axes, "head"),
        P(axes, None),
        P(None, "head"),
        P(None, "head"),
        P(axes, "head"),
        P(),
    )
    return jax.shard_map(
        local,
        mesh=Mesh(devices, (*axes, "head")),
        in_specs=placed,
        out_specs=(P(axes, "head"), P(axes, None), P(axes, "head"), P(axes, "head")),
        check_vma=False,
    )
```

```python
import math

import jax
import jax.numpy as jnp
from jax import lax
from jax.experimental import pallas as pl
from jax.experimental.pallas import tpu as pltpu
from jax.sharding import Mesh
from jax.sharding import PartitionSpec as P

LATENT = 512
ROPE = 64
NOPE = 128
VDIM = 128
WIDTH_Q = NOPE + ROPE
HALF = 64
BLOCKS = 64
HEADS = 4
SIDE = 4
CHIPS = SIDE * SIDE
PIECE = HALF // 2
ROWS = 2 * HALF
KEYS = 2 * CHIPS * HALF
QUERIES = 2 * CHIPS * PIECE
KEY_ROWS = 2 * HALF + PIECE
IN_ROWS = KEY_ROWS + 5 * PIECE
OUT_ROWS = KEY_ROWS + 3 * PIECE
W_ROWS = LATENT // (2 * CHIPS)
W_WIDTH = HEADS * (NOPE + VDIM)
CHUNK = 1024
GROUP = 512
N_CHUNKS = KEYS // CHUNK
N_GROUPS = QUERIES // GROUP
UNROLL = CHIPS
Z_WIDTH = 640
LOG2E = 1.4426950408889634
SCALE = 1.0 / math.sqrt(WIDTH_Q)

eps = 1e-06
masked_low = -1e30
bf16 = jnp.bfloat16
f32 = jnp.float32
VMEM = pl.BlockSpec(memory_space=pltpu.VMEM)
SMEM = pl.BlockSpec(memory_space=pltpu.SMEM)
ANY = pl.BlockSpec(memory_space=pl.ANY)


def dot(left, right, left_dim=1, right_dim=0):
    return lax.dot_general(
        left, right, (((left_dim,), (right_dim,)), ((), ())), preferred_element_type=f32
    )


def rms_rows(latent):
    values = latent.astype(f32)
    inverse = lax.rsqrt(jnp.mean(values * values, axis=-1, keepdims=True) + eps)
    return (values * inverse, inverse)


def list_blocks(starts, meta, q_pos):
    half = lax.axis_index("y") % 2
    core = lax.axis_index("core")
    shape = (BLOCKS, BLOCKS)
    across = jnp.broadcast_to(starts[...], shape)
    down = across.T
    row = lax.broadcasted_iota(jnp.int32, shape, 0)
    lane = lax.broadcasted_iota(jnp.int32, shape, 1)

    def tally(where, axis):
        return jnp.sum(where.astype(jnp.int32), axis=axis, keepdims=True)

    key_rank = tally((down < across) & (row % 2 == half), 0)
    query_rank = tally((down < across) & ((row // 2) % 2 == core), 0)
    query_rank_down = tally((across < down) & ((lane // 2) % 2 == core), 1)
    is_query = (row[:, :1] // 2) % 2 == core
    shape = (BLOCKS, QUERIES)
    piece = lax.broadcasted_iota(jnp.int32, shape, 1) // PIECE
    mine = (query_rank_down == piece) & is_query
    position = jnp.sum(jnp.where(mine, down[:, :1], 0), axis=0, keepdims=True)
    seen = []
    for group in range(N_GROUPS):
        last = position[:, (group + 1) * GROUP - 1 : (group + 1) * GROUP]
        seen.append(tally((across[:1] <= last) & (lane[:1] % 2 == half), 1))
    seen = jnp.concatenate(seen + [jnp.zeros((1, BLOCKS - N_GROUPS), jnp.int32)], axis=1)
    rest = jnp.zeros((5, BLOCKS), jnp.int32)
    meta[...] = jnp.concatenate([key_rank, query_rank, seen, rest], axis=0)
    offset = lax.broadcasted_iota(jnp.int32, (1, QUERIES), 1) % PIECE
    offset = offset + (lax.axis_index("y") // 2) * PIECE
    q_pos[...] = jnp.broadcast_to(position + offset, q_pos.shape)


def pack_kernel(
    block_start,
    kv_any,
    wk_any,
    wv_any,
    q_any,
    g_any,
    out_any,
    meta,
    q_pos,
    kv_ref,
    wk_ref,
    wv_ref,
    q_ref,
    g_ref,
    out_ref,
    sems,
    out_sems,
):
    pairs = [(q_any, q_ref), (g_any, g_ref), (kv_any, kv_ref), (wk_any, wk_ref), (wv_any, wv_ref)]
    copies = [
        pltpu.make_async_copy(source, target, sems.at[index])
        for index, (source, target) in enumerate(pairs)
    ]
    for copy in reversed(copies):
        copy.start()
    list_blocks(block_start, meta, q_pos)
    copies[0].wait()
    copies[1].wait()
    for x in range(HEADS):
        q_nope = q_ref[:, x * WIDTH_Q : x * WIDTH_Q + NOPE]
        q_rope = q_ref[:, x * WIDTH_Q + NOPE : (x + 1) * WIDTH_Q]
        grad = g_ref[:, x * VDIM : (x + 1) * VDIM]
        for y in range(SIDE):
            slot = y * SIDE + x
            first = slice((y // 2) * PIECE, (y // 2 + 1) * PIECE)
            second = slice(HALF + (y // 2) * PIECE, HALF + (y // 2 + 1) * PIECE)
            low = KEY_ROWS
            out_ref[slot, low : low + PIECE] = q_nope[first]
            out_ref[slot, low + PIECE : low + 2 * PIECE] = q_nope[second]
            out_ref[slot, low + 2 * PIECE : low + 3 * PIECE] = grad[first]
            out_ref[slot, low + 3 * PIECE : low + 4 * PIECE] = grad[second]
            out_ref[slot, low + 4 * PIECE : low + 5 * PIECE] = jnp.concatenate(
                [q_rope[first], q_rope[second]], axis=1
            )
    part = (slice(None), pl.ds(KEY_ROWS, IN_ROWS - KEY_ROWS))
    sent = [pltpu.make_async_copy(out_ref.at[part], out_any.at[part], out_sems.at[SIDE])]
    sent[0].start()
    copies[2].wait()
    values = kv_ref[:LATENT, :].astype(f32)
    inverse = lax.rsqrt(jnp.mean(values * values, axis=0, keepdims=True) + eps)
    normed = (values * inverse).T.astype(bf16)
    rope = kv_ref[LATENT:, :].astype(f32).T.astype(bf16)
    copies[3].wait()
    keys = dot(normed, wk_ref[...]).astype(bf16)
    copies[4].wait()
    values = dot(normed, wv_ref[...]).astype(bf16)
    for y in range(SIDE):
        low = (y % 2) * HALF
        for x in range(HEADS):
            slot = y * SIDE + x
            out_ref[slot, :HALF] = keys[low : low + HALF, x * NOPE : (x + 1) * NOPE]
            out_ref[slot, HALF : 2 * HALF] = values[low : low + HALF, x * VDIM : (x + 1) * VDIM]
            out_ref[slot, 2 * HALF : KEY_ROWS] = jnp.concatenate(
                [rope[low : low + PIECE], rope[low + PIECE : low + HALF]], axis=1
            )
        part = (pl.ds(y * SIDE, SIDE), pl.ds(0, KEY_ROWS))
        sent.append(pltpu.make_async_copy(out_ref.at[part], out_any.at[part], out_sems.at[y]))
        sent[-1].start()
    for copy in sent:
        copy.wait()


def key_block(chip, core):
    return (2 * chip + core) * 2 + lax.axis_index("y") % 2


def place_positions(block_start, meta, k_pos):
    rows = lax.broadcasted_iota(jnp.int32, (HALF, NOPE), 0)

    def body(index, carry):
        block = 2 * index + lax.axis_index("y") % 2
        at = pl.ds(pl.multiple_of(meta[0, block] * HALF, HALF), HALF)
        k_pos[at, :] = rows + block_start[block]
        return carry

    lax.fori_loop(0, 2 * CHIPS, body, 0, unroll=UNROLL)


def step_rows(group):
    return CHUNK // 2 if group == 0 else CHUNK


def seen_steps(meta, group):
    return (meta[2, group] * HALF + step_rows(group) - 1) // step_rows(group)


def place_kernel(block_start, meta, own_ref, queries, grads, k_pos):
    core = lax.axis_index("core")
    pad = jnp.zeros((PIECE, HALF), bf16)

    def place(chip, carry):
        low = KEY_ROWS
        q_rope = own_ref[chip, low + 4 * PIECE : low + 5 * PIECE]
        for half in range(2):
            rank = meta[1, (2 * chip + core) * 2 + half]
            at = pl.ds(pl.multiple_of(rank * PIECE, PIECE), PIECE)
            queries[at, :NOPE] = own_ref[chip, low + half * PIECE : low + (half + 1) * PIECE]
            queries[at, NOPE:] = jnp.concatenate(
                [q_rope[:, half * HALF : (half + 1) * HALF], pad], axis=1
            )
            grads[at, :] = own_ref[chip, low + (2 + half) * PIECE : low + (3 + half) * PIECE]
        return carry

    lax.fori_loop(0, CHIPS, place, 0, unroll=UNROLL)
    place_positions(block_start, meta, k_pos)


def stats_kernel(
    meta,
    q_pos,
    own_ref,
    other_ref,
    queries,
    grads,
    k_pos,
    keys,
    stats,
    scores,
    slopes,
    values,
):
    core = lax.axis_index("core")
    pad = jnp.zeros((HALF, HALF), bf16)

    def place(chip, carry):
        for ref, side in ((own_ref, core), (other_ref, 1 - core)):
            rank = meta[0, key_block(chip, side)]
            at = pl.ds(pl.multiple_of(rank * HALF, HALF), HALF)
            rope = ref[chip, 2 * HALF : KEY_ROWS]
            rope = jnp.concatenate([rope[:, :HALF], rope[:, HALF:]], axis=0)
            keys[at, :NOPE] = ref[chip, :HALF]
            keys[at, NOPE:] = jnp.concatenate([rope, pad], axis=1)
            values[at, :] = ref[chip, HALF : 2 * HALF]
        return carry

    lax.fori_loop(0, CHIPS, place, 0, unroll=UNROLL)

    for group in range(N_GROUPS):
        lanes = slice(group * GROUP, (group + 1) * GROUP)
        q_group = queries[lanes, :]
        g_group = grads[lanes, :]
        q_at = q_pos[0:1, lanes]

        rows = step_rows(group)

        def gather_stats(index, carry, lanes=lanes, rows=rows):
            top, weight_sum, weighted = carry
            at = pl.ds(pl.multiple_of(index * rows, rows), rows)
            score = dot(keys[at, :], q_group, 1, 1) * (SCALE * LOG2E)
            key_at = jnp.concatenate([k_pos[at, :]] * (GROUP // NOPE), axis=1)
            score = jnp.where(key_at <= q_at, score, masked_low)
            slope = dot(values[at, :], g_group, 1, 1)
            scores[at, lanes] = score
            slopes[at, lanes] = slope
            fresh = jnp.maximum(top, jnp.max(score, axis=0, keepdims=True))
            fade = jnp.exp2(top - fresh)
            weight = jnp.exp2(score - fresh)
            weight_sum = weight_sum * fade + jnp.sum(weight, axis=0, keepdims=True)
            weighted = weighted * fade + jnp.sum(weight * slope, axis=0, keepdims=True)
            return (fresh, weight_sum, weighted)

        zero = jnp.zeros((1, GROUP), f32)
        top, weight_sum, weighted = lax.fori_loop(
            0,
            seen_steps(meta, group),
            gather_stats,
            (jnp.full((1, GROUP), masked_low, f32), zero, zero),
        )
        stats[:, lanes] = jnp.concatenate(
            [top, weight_sum, weighted, jnp.zeros((5, GROUP), f32)], axis=0
        )


def gradient_kernel(
    meta,
    keys,
    queries,
    grads,
    scores,
    slopes,
    own_stats,
    other_stats,
    own_out,
    other_out,
    key_grads,
    value_grads,
    query_grads,
    key_sum,
    value_sum,
):
    own_top = own_stats[0:1, :]
    other_top = other_stats[0:1, :]
    top = jnp.maximum(own_top, other_top)
    own_fade = jnp.exp2(own_top - top)
    other_fade = jnp.exp2(other_top - top)
    weight_sum = own_stats[1:2, :] * own_fade + other_stats[1:2, :] * other_fade
    weighted = own_stats[2:3, :] * own_fade + other_stats[2:3, :] * other_fade
    log_scaled = top + jnp.log2(weight_sum) - math.log2(SCALE)
    average = weighted / weight_sum
    query_grads[...] = jnp.zeros_like(query_grads)

    def gradients(index, carry):
        at = pl.ds(pl.multiple_of(index * CHUNK, CHUNK), CHUNK)
        key_sum[...] = jnp.zeros_like(key_sum)
        value_sum[...] = jnp.zeros_like(value_sum)
        for group in range(N_GROUPS):
            lanes = slice(group * GROUP, (group + 1) * GROUP)
            rows = step_rows(group)
            for step in range(CHUNK // rows):

                @pl.when(index * (CHUNK // rows) + step < seen_steps(meta, group))
                def _(lanes=lanes, rows=rows, step=step):
                    part = slice(step * rows, (step + 1) * rows)
                    at = pl.ds(pl.multiple_of(index * CHUNK + step * rows, rows), rows)
                    probs = jnp.exp2(scores[at, lanes] - log_scaled[:, lanes])
                    score_grad = (probs * (slopes[at, lanes] - average[:, lanes])).astype(bf16)
                    value_sum[part, :] += dot(probs.astype(bf16), grads[lanes, :])
                    key_sum[part, :] += dot(score_grad, queries[lanes, :])
                    query_grads[lanes, :] += dot(score_grad, keys[at, :], 0, 0)

        key_grads[at, :] = key_sum[...].astype(bf16)
        value_grads[at, :] = (value_sum[...] * (1.0 / SCALE)).astype(bf16)
        return carry

    lax.fori_loop(0, N_CHUNKS, gradients, 0)
    core = lax.axis_index("core")

    def hand_out(chip, carry):
        for ref, side in ((own_out, core), (other_out, 1 - core)):
            rank = meta[0, key_block(chip, side)]
            at = pl.ds(pl.multiple_of(rank * HALF, HALF), HALF)
            ref[chip, :HALF] = key_grads[at, :NOPE]
            ref[chip, HALF : 2 * HALF] = value_grads[at, :]
            rope = key_grads[at, NOPE:WIDTH_Q]
            ref[chip, 2 * HALF : KEY_ROWS] = jnp.concatenate([rope[:PIECE], rope[PIECE:]], axis=1)
        low = KEY_ROWS
        ropes = []
        for half in range(2):
            rank = meta[1, (2 * chip + core) * 2 + half]
            at = pl.ds(pl.multiple_of(rank * PIECE, PIECE), PIECE)
            piece = query_grads[at, :].astype(bf16)
            own_out[chip, low + half * PIECE : low + (half + 1) * PIECE] = piece[:, :NOPE]
            ropes.append(piece[:, NOPE:WIDTH_Q])
        own_out[chip, low + 2 * PIECE : low + 3 * PIECE] = jnp.concatenate(ropes, axis=1)
        return carry

    lax.fori_loop(0, CHIPS, hand_out, 0, unroll=UNROLL)


def slot_sum(slots_ref, slots, low, rows):
    total = slots_ref[slots[0], low : low + rows].astype(f32)
    for slot in slots[1:]:
        total = total + slots_ref[slot, low : low + rows].astype(f32)
    return total


def head_sums(slots_ref, low):
    parts = []
    for x in range(HEADS):
        halves = [
            slot_sum(slots_ref, (y * SIDE + x, (y + 2) * SIDE + x), low, HALF) for y in range(2)
        ]
        parts.append(jnp.concatenate(halves, axis=0).astype(bf16))
    return jnp.concatenate(parts, axis=1)


def latent_kernel(
    slots_ref, wk_ref, wv_ref, kv_ref, out_ref, grad_q_ref, own_ref, other_ref, terms
):
    key_flat = head_sums(slots_ref, 0)
    value_flat = head_sums(slots_ref, HALF)
    latent = dot(key_flat, wk_ref[...], 1, 1) + dot(value_flat, wv_ref[...], 1, 1)
    out_ref[:, :LATENT] = latent.astype(bf16)
    ropes = []
    for y in range(2):
        slots = [row * SIDE + x for row in (y, y + 2) for x in range(HEADS)]
        rope = slot_sum(slots_ref, slots, 2 * HALF, PIECE)
        ropes += [rope[:, :HALF], rope[:, HALF:]]
    rope = jnp.concatenate(ropes, axis=0)
    out_ref[:, LATENT:] = jnp.concatenate([rope, jnp.zeros_like(rope)], axis=1).astype(bf16)
    values = kv_ref[:LATENT, :].astype(f32)
    inverse = lax.rsqrt(jnp.mean(values * values, axis=0, keepdims=True) + eps)
    normed = (values * inverse).astype(bf16)
    terms[:, : HEADS * NOPE] = dot(normed, key_flat).astype(bf16)
    terms[:, HEADS * NOPE :] = dot(normed, value_flat).astype(bf16)
    core = lax.axis_index("core")
    y_here, x_here = lax.axis_index("y"), lax.axis_index("x")
    for dx in range(SIDE):
        for dy in range(SIDE):
            chip = (y_here ^ dy) * SIDE + (x_here ^ dx)
            first = pl.multiple_of((2 * chip + core) * W_ROWS, W_ROWS)
            second = pl.multiple_of((2 * chip + 1 - core) * W_ROWS, W_ROWS)
            own_ref[dx, dy] = terms[pl.ds(first, W_ROWS), :]
            other_ref[dx, dy] = terms[pl.ds(second, W_ROWS), :]
    low = KEY_ROWS
    for quarter in range(2):
        for half in range(2):
            parts = []
            for x in range(HEADS):
                slots = (2 * quarter * SIDE + x, (2 * quarter + 1) * SIDE + x)
                parts.append(slot_sum(slots_ref, slots, low + half * PIECE, PIECE))
                rope = slot_sum(slots_ref, slots, low + 2 * PIECE, PIECE)
                parts.append(rope[:, half * HALF : (half + 1) * HALF])
            first = half * HALF + quarter * PIECE
            grad_q_ref[first : first + PIECE, :] = jnp.concatenate(parts, axis=1).astype(bf16)


def norm_kernel(slots_ref, kv_ref, out_ref):
    total = jnp.sum(slots_ref[...].astype(f32), axis=0)
    x_hat, inverse = rms_rows(kv_ref[:, :LATENT])
    latent = total[:, :LATENT]
    latent = inverse * (latent - x_hat * jnp.mean(latent * x_hat, axis=-1, keepdims=True))
    row = jnp.concatenate([latent, total[:, LATENT:]], axis=1).astype(bf16)
    out_ref[...] = jnp.broadcast_to(row[None], out_ref.shape)


def call(kernel, shapes, specs, scratch=(), limit=32, flops=0, moved=0, out_specs=None):
    shapes = [jax.ShapeDtypeStruct(*shape) for shape in shapes]
    single = len(shapes) == 1
    if out_specs is None:
        out_specs = VMEM if single else [VMEM] * len(shapes)
    return pl.pallas_call(
        kernel,
        out_shape=shapes[0] if single else shapes,
        in_specs=specs,
        out_specs=out_specs,
        scratch_shapes=scratch,
        compiler_params=pltpu.CompilerParams(vmem_limit_bytes=limit * 2**20),
        cost_estimate=pl.CostEstimate(flops=flops, bytes_accessed=moved, transcendentals=0),
    )


def run_pack(*args):
    return call(
        pack_kernel,
        [
            ((CHIPS, IN_ROWS, NOPE), bf16),
            ((8, BLOCKS), jnp.int32),
            ((8, QUERIES), jnp.int32),
        ],
        [VMEM] + [ANY] * 5,
        [
            pltpu.VMEM((LATENT + ROPE, ROWS), bf16),
            pltpu.VMEM((LATENT, HEADS * NOPE), bf16),
            pltpu.VMEM((LATENT, HEADS * VDIM), bf16),
            pltpu.VMEM((ROWS, HEADS * WIDTH_Q), bf16),
            pltpu.VMEM((ROWS, HEADS * VDIM), bf16),
            pltpu.VMEM((CHIPS, IN_ROWS, NOPE), bf16),
            pltpu.SemaphoreType.DMA((5,)),
            pltpu.SemaphoreType.DMA((SIDE + 1,)),
        ],
        limit=60,
        out_specs=[ANY, VMEM, VMEM],
    )(*args)


def run_place(*args):
    return call(
        place_kernel,
        [((QUERIES, 2 * NOPE), bf16), ((QUERIES, VDIM), bf16), ((KEYS, NOPE), jnp.int32)],
        [SMEM] * 2 + [VMEM],
        limit=16,
        flops=10**8,
        moved=4 * 2**20,
    )(*args)


def run_stats(*args):
    return call(
        stats_kernel,
        [
            ((KEYS, 2 * NOPE), bf16),
            ((8, QUERIES), f32),
            ((KEYS, QUERIES), f32),
            ((KEYS, QUERIES), f32),
        ],
        [SMEM] + [VMEM] * 6,
        [pltpu.VMEM((KEYS, VDIM), bf16)],
        limit=28,
    )(*args)


def run_gradient(*args):
    return call(
        gradient_kernel,
        [((CHIPS, OUT_ROWS, NOPE), bf16), ((CHIPS, KEY_ROWS, NOPE), bf16)],
        [SMEM] + [VMEM] * 7,
        [
            pltpu.VMEM((KEYS, 2 * NOPE), bf16),
            pltpu.VMEM((KEYS, VDIM), bf16),
            pltpu.VMEM((QUERIES, 2 * NOPE), f32),
            pltpu.VMEM((CHUNK, 2 * NOPE), f32),
            pltpu.VMEM((CHUNK, VDIM), f32),
        ],
        limit=28,
    )(*args)


def over_chips(slots):
    return lax.all_to_all(slots, ("y", "x"), 0, 0)


def swap(array, axis, bit):
    return lax.ppermute(array, axis, [(i, i ^ bit) for i in range(lax.axis_size(axis))])


def local(query, kv_row, w_uk, w_uv, grad_out, block_start):
    z_size = lax.axis_size("head")
    z_rows = ROWS // z_size
    kv_t = kv_row.T
    slots, meta, q_pos = run_pack(
        block_start.reshape(1, BLOCKS), kv_t, w_uk, w_uv, query, grad_out
    )
    own = over_chips(slots)
    other = swap(own[:, :KEY_ROWS], "core", 1)

    queries, grads, k_pos = run_place(block_start, meta, own)
    keys, stats, scores, slopes = run_stats(meta, q_pos, own, other, queries, grads, k_pos)
    own_part, other_part = run_gradient(
        meta, keys, queries, grads, scores, slopes, stats, swap(stats, "y", 1)
    )
    slots = over_chips(own_part.at[:, :KEY_ROWS].add(swap(other_part, "core", 1)))

    z_part, grad_query, own_terms, other_terms = call(
        latent_kernel,
        [((ROWS, Z_WIDTH), bf16), ((ROWS, HEADS * WIDTH_Q), bf16)]
        + [((SIDE, SIDE, W_ROWS, W_WIDTH), bf16)] * 2,
        [VMEM] * 4,
        [pltpu.VMEM((LATENT, W_WIDTH), bf16)],
    )(slots, w_uk, w_uv, kv_t)
    terms = own_terms + swap(other_terms, "core", 1)
    for axis in ("x", "y"):
        total = terms[0].astype(f32)
        for bit in (3, 2, 1):
            total = total + swap(terms[bit], axis, bit).astype(f32)
        terms = total.astype(bf16)

    z_slots = lax.all_to_all(z_part.reshape(z_size, z_rows, Z_WIDTH), "head", 0, 0)
    first_row = lax.axis_index("head") * z_rows
    kv_rows = lax.dynamic_slice_in_dim(kv_row, first_row, z_rows)
    rows = call(norm_kernel, [((z_size, z_rows, Z_WIDTH), bf16)], [VMEM] * 2)(z_slots, kv_rows)
    all_rows = lax.all_to_all(rows, "head", 0, 0).reshape(ROWS, Z_WIDTH)
    grad_kv_row = all_rows[:, : LATENT + ROPE].astype(f32)
    width = HEADS * NOPE
    return (grad_query, grad_kv_row, total[:, :width], total[:, width:])


def solution(mesh):
    axes = ("y", "x", "core")
    devices = mesh.devices.reshape(SIDE, SIDE, 2, mesh.shape["head"])
    placed = (
        P(axes, "head"),
        P(axes, None),
        P(None, "head"),
        P(None, "head"),
        P(axes, "head"),
        P(),
    )
    return jax.shard_map(
        local,
        mesh=Mesh(devices, (*axes, "head")),
        in_specs=placed,
        out_specs=(P(axes, "head"), P(axes, None), P(axes, "head"), P(axes, "head")),
        check_vma=False,
    )
```
